512 devices in a mesh: pair: 16 (over x_hi, y, core), row: 32 (over x_lo, z).
Axes of the slice: x: 4 (x_hi: 2, x_lo: 2; x = x_hi * 2 + x_lo), y: 4, z: 16, core: 2. Of those that a mesh axis runs over, the one named last changes fastest.
Arguments:
- snapshots: float32 [4096, 8192], P('row', 'pair'), may hold values from -60 to 60
Outputs:
- rotated: float32 [4096, 8192], P('row', 'pair')
The draws below stay inside these ranges and needn't reach their ends.
All inputs are finite; a program needn't handle non-finite values.
Results may differ from the reference program's by a relative error of at most 0.0003.
Values sent between devices are 32-bit elements; how exact they have to be, the bound alone decides.
No kernel may reach another device: no remote copies, remote signals or barrier semaphores. Data moves between devices by JAX's collectives and lax.ppermute only.
A program may use at most 64 MiB of HBM per device.

```python
import math
import jax
import jax.numpy as jnp
import numpy as np
from jax import lax

B = 256
STEPS = 3
ROUNDS = 3
PAIRS = 16
ROWS = 4096
COLS = 8192


def draw_snapshots(key, part):
    key = jax.random.fold_in(key, 7)
    first_key, second_key = jax.random.split(key, 2)
    base_field = jnp.clip(jax.random.normal(first_key, (ROWS, COLS), jnp.float32), -5.0, 5.0)
    mixed = base_field + 0.6 * (jnp.roll(base_field, B + 1, axis=1) + jnp.roll(base_field, 4 * B + 4, axis=1) + jnp.roll(base_field, 5 * B + 5, axis=1))
    column_scale = jnp.exp(jax.random.uniform(second_key, (1, COLS), jnp.float32, math.log(0.3), math.log(3.0)))
    return (mixed * column_scale).astype(jnp.float32)


def setup_inputs(seed: int = 0) -> dict:
    streams_of = jax.random.split(jax.random.key(seed), 2)
    return {
        "snapshots": draw_snapshots(jax.random.fold_in(streams_of[1], 71), 0),
    }


def round_robin(order_size, section_count):
    players = list(range(order_size))
    orders = []
    half_size = order_size // 2
    for section_index in range(section_count):
        layout = [players[position_i] for position_i in range(half_size)] + [players[order_size - 1 - position_i] for position_i in range(half_size)]
        orders.append(np.array(layout, dtype=np.int32))
        players = [players[0], players[-1]] + players[1:-1]
    return orders

def angles(current):
    half_size = current.shape[0] // 2
    diagonal = jnp.diagonal(current)
    upper_diag = diagonal[:half_size]
    lower_diag = diagonal[half_size:]
    coupling = jnp.diagonal(current[:half_size, half_size:])
    difference = lower_diag - upper_diag
    sign_term = jnp.where(difference >= 0, 1.0, -1.0)
    radius = jnp.sqrt(difference * difference + 4.0 * coupling * coupling + (1e-06 * (upper_diag + lower_diag)) ** 2)
    tangent = 2.0 * coupling * sign_term / (jnp.abs(difference) + radius)
    cosine = 1.0 / jnp.sqrt(1.0 + tangent * tangent)
    return (cosine, tangent * cosine)

def turn_rows(matrix, cosine, sine_term):
    half_size = matrix.shape[0] // 2
    leading = matrix[:half_size]
    second = matrix[half_size:]
    return jnp.concatenate([cosine[:, None] * leading - sine_term[:, None] * second, sine_term[:, None] * leading + cosine[:, None] * second], axis=0)

def turn_cols(matrix, cosine, sine_term):
    half_size = matrix.shape[1] // 2
    leading = matrix[:, :half_size]
    second = matrix[:, half_size:]
    return jnp.concatenate([cosine[None, :] * leading - sine_term[None, :] * second, sine_term[None, :] * leading + cosine[None, :] * second], axis=1)

def diagonalize(gram_matrix):
    order_size = gram_matrix.shape[0]
    orders = round_robin(order_size, STEPS)
    current = gram_matrix[orders[0]][:, orders[0]]
    frame_basis = jnp.eye(order_size, dtype=gram_matrix.dtype)[:, orders[0]]
    for sweep_step in range(STEPS):
        if sweep_step > 0:
            relative = np.argsort(orders[sweep_step - 1])[orders[sweep_step]]
            current = current[relative][:, relative]
            frame_basis = frame_basis[:, relative]
        cosine, sine_term = angles(current)
        current = turn_cols(turn_rows(current, cosine, sine_term), cosine, sine_term)
        frame_basis = turn_cols(frame_basis, cosine, sine_term)
    restore = np.argsort(orders[-1])
    return (frame_basis[:, restore], current[restore][:, restore])

def one_pair(work_block):
    gram_matrix = jnp.einsum('ra,rb->ab', work_block, work_block, precision=lax.Precision.HIGHEST)
    frame_basis, turned = diagonalize(gram_matrix)
    return jnp.dot(work_block, frame_basis, precision=lax.Precision.HIGHEST)

def reference(snapshots):
    blocks = snapshots.reshape(ROWS, PAIRS, 2 * B).transpose(1, 0, 2)
    for round_index in range(ROUNDS):
        turned_blocks = lax.map(one_pair, blocks)
        upper_part = turned_blocks[:, :, :B]
        lower_part = turned_blocks[:, :, B:]
        new_upper = jnp.concatenate([upper_part[:1], lower_part[:1], upper_part[1:-1]], axis=0)
        new_lower = jnp.concatenate([lower_part[1:], upper_part[-1:]], axis=0)
        blocks = jnp.concatenate([new_upper, new_lower], axis=2)
    return blocks.transpose(1, 0, 2).reshape(ROWS, COLS)
```

```python
import functools

import jax
import jax.numpy as jnp
from jax import lax
from jax.experimental import pallas as pl
from jax.experimental.pallas import tpu as pltpu
from jax.sharding import Mesh, PartitionSpec as P

HALF = 256
LANES = 128
BANDS = 11
PACKED_ROWS = 24
CHUNK = 8


def lanes_of(x):
    return lax.broadcasted_iota(jnp.int32, x.shape, 1)


def roll(x, by):
    return pltpu.roll(x, by % HALF, 1)


def before(x):
    return jnp.where(lanes_of(x) == 0, x, roll(x, 1))


def after(x):
    return jnp.where(lanes_of(x) == HALF - 1, x, roll(x, -1))


def far_before(x):
    lane = lanes_of(x)
    return jnp.where(lane == 0, roll(x, -1), jnp.where(lane == 1, roll(x, 1), roll(x, 2)))


def far_after(x):
    lane = lanes_of(x)
    return jnp.where(
        lane == HALF - 1, roll(x, 1), jnp.where(lane == HALF - 2, roll(x, -1), roll(x, -2))
    )


def advance(top, bottom):
    lane = lanes_of(top)
    new_top = jnp.where(lane == 0, top, roll(jnp.where(lane == 0, bottom, top), 1))
    new_bottom = jnp.where(lane == HALF - 1, top, roll(bottom, -1))
    return new_top, new_bottom


def retreat(top, bottom):
    lane = lanes_of(top)
    rolled = roll(top, -1)
    old_top = jnp.where(lane == 0, top, jnp.where(lane == HALF - 1, bottom, rolled))
    old_bottom = jnp.where(lane == 0, rolled, roll(bottom, 1))
    return old_top, old_bottom


def turn(top, bottom, cosine, sine):
    return cosine * top - sine * bottom, sine * top + cosine * bottom


def reverse(x):
    index = LANES - 1 - lax.broadcasted_iota(jnp.int32, (x.shape[0], LANES), 1)
    flip = lambda part: jnp.take_along_axis(part, index, axis=1)
    return jnp.concatenate([flip(x[:, LANES:]), flip(x[:, :LANES])], axis=1)


def band_products(top, bottom):
    top_m, bottom_m, top_n, bottom_n = before(top), before(bottom), after(top), after(bottom)
    top_f, bottom_f = far_before(top), far_before(bottom)
    top_g, bottom_g = far_after(top), far_after(bottom)
    return (
        top * top, bottom * bottom, top * bottom,
        top_m * top_n, top_m * bottom_n, bottom_m * top_n, bottom_m * bottom_n,
        top_f * top_g, top_f * bottom_g, bottom_f * top_g, bottom_f * bottom_g,
    )


def bands_of(read, rows):
    total = None
    for start in range(0, rows, CHUNK):
        terms = band_products(*read(start))
        total = terms if total is None else [t + u for t, u in zip(total, terms)]
    sums = [jnp.sum(t, axis=0, keepdims=True) for t in total]
    blank = jnp.zeros((PACKED_ROWS - 2 * BANDS, LANES), jnp.float32)
    return jnp.concatenate(
        [s[:, :LANES] for s in sums] + [s[:, LANES:] for s in sums] + [blank], axis=0
    )


def angles(a, b, c):
    difference = b - a
    sign = jnp.where(difference >= 0, 1.0, -1.0)
    radius = jnp.sqrt(difference * difference + 4.0 * c * c + (1e-06 * (a + b)) ** 2)
    tangent = 2.0 * c * sign / (jnp.abs(difference) + radius)
    cosine = 1.0 / jnp.sqrt(1.0 + tangent * tangent)
    return cosine, tangent * cosine


def turn_diagonal(a, b, c, cosine, sine):
    cc, ss, cs = cosine * cosine, sine * sine, cosine * sine
    twice = 2.0 * cs * c
    return cc * a - twice + ss * b, ss * a + twice + cc * b, cs * (a - b) + (cc - ss) * c


def turn_block(block, left, right):
    pp, pq, qp, qq = block
    pp, qp = turn(pp, qp, *left)
    pq, qq = turn(pq, qq, *left)
    pp, pq = turn(pp, pq, *right)
    qp, qq = turn(qp, qq, *right)
    return pp, pq, qp, qq


def three_angles(packed):
    rows = [
        jnp.concatenate([packed[k : k + 1], packed[BANDS + k : BANDS + k + 1]], axis=1)
        for k in range(BANDS)
    ]
    a, b, c = rows[:3]
    lane = lanes_of(a)
    last = HALF - 1
    first = angles(a, b, c)
    a, b, c = turn_diagonal(a, b, c, *first)
    both = lambda move, pair: (move(pair[0]), move(pair[1]))
    near_pp, near_pq, near_qp, near_qq = turn_block(
        rows[3:7], both(before, first), both(after, first)
    )
    far_pp, far_pq, _, far_qq = turn_block(
        rows[7:11], both(far_before, first), both(far_after, first)
    )
    a, b = advance(a, b)
    cross = jnp.where(lane == 1, near_qq, jnp.where(lane == last, near_pp, near_pq))
    second = angles(a, b, cross)
    a, b, _ = turn_diagonal(a, b, cross, *second)
    pp = jnp.where(
        lane == 0, c, jnp.where(lane == 2, roll(near_qp, 1), jnp.where(lane == last, far_pp, roll(near_pp, 1)))
    )
    qq = jnp.where(
        lane == 0,
        far_qq,
        jnp.where(lane == last - 1, roll(near_qp, -1), jnp.where(lane == last, c, roll(near_qq, -1))),
    )
    pq = jnp.where(
        lane == 0,
        roll(near_pq, -1),
        jnp.where(
            lane == 2,
            far_qq,
            jnp.where(lane == last - 1, far_pp, jnp.where(lane == last, roll(near_pp, 1), far_pq)),
        ),
    )
    qp = jnp.where(lane == 0, near_qq, jnp.where(lane == last, near_pq, c))
    pp, pq, _, qq = turn_block((pp, pq, qp, qq), both(before, second), both(after, second))
    a, b = advance(a, b)
    cross = jnp.where(lane == 1, qq, jnp.where(lane == last, pp, pq))
    return first, second, angles(a, b, cross)


def ordered_sum(x):
    return functools.reduce(jnp.add, [x[i] for i in range(x.shape[0])])


def chosen(condition, x, y):
    return jnp.where(condition, x, y)


def wide(angle_pairs):
    return [[jnp.broadcast_to(v, (CHUNK, HALF)) for v in pair] for pair in angle_pairs]


def rotated(top, bottom, angle_pairs):
    first, second, third = angle_pairs
    top, bottom = advance(*turn(top, bottom, *first))
    top, bottom = advance(*turn(top, bottom, *second))
    top, bottom = turn(top, bottom, *third)
    return retreat(*retreat(top, bottom))


def chunks(ref):
    return [pl.ds(start, CHUNK) for start in range(0, ref.shape[0], CHUNK)]


def start_kernel(work_ref, top_ref, bottom_ref, band_ref):
    def read(start):
        row = pl.ds(start, CHUNK)
        top = work_ref[row, :HALF]
        bottom = reverse(work_ref[row, HALF:])
        top_ref[row, :] = top
        bottom_ref[row, :] = bottom
        return top, bottom

    band_ref[...] = bands_of(read, work_ref.shape[0])


def rotate_kernel(place_ref, top_ref, bottom_ref, parts_ref, kept_ref, odd_ref, even_ref):
    place = place_ref[0, 0]
    at_odd = place % 2 == 1
    angle_pairs = wide(three_angles(ordered_sum(parts_ref)))
    for row in chunks(top_ref):
        top, bottom = rotated(top_ref[row, :], bottom_ref[row, :], angle_pairs)
        right = chosen(place == 0, reverse(bottom), top)
        kept_ref[row, :] = chosen(place == 0, top, reverse(top))
        odd_ref[row, :] = chosen(at_odd, right, bottom)
        even_ref[row, :] = chosen(at_odd, bottom, right)


def arrive_kernel(count, place_ref, kept_ref, odd_ref, even_ref, top_ref, bottom_ref, band_ref):
    place = place_ref[0, 0]
    at_odd = place % 2 == 1

    def read(start):
        row = pl.ds(start, CHUNK)
        kept, odd, even = kept_ref[row, :], odd_ref[row, :], even_ref[row, :]
        top = chosen(place == 0, kept, chosen(at_odd, even, odd))
        bottom = chosen(place == count - 1, kept, chosen(at_odd, odd, even))
        top_ref[row, :] = top
        bottom_ref[row, :] = bottom
        return top, bottom

    band_ref[...] = bands_of(read, kept_ref.shape[0])


def rotate_far_kernel(count, place_ref, top_ref, bottom_ref, parts_ref, x_ref, y_ref):
    place = place_ref[0, 0]
    low = place % 4 < 2
    angle_pairs = wide(three_angles(ordered_sum(parts_ref)))
    for row in chunks(top_ref):
        top, bottom = rotated(top_ref[row, :], bottom_ref[row, :], angle_pairs)
        flip = reverse(chosen(place == 0, bottom, top))
        upper = chosen((place == 0) | (place == count - 1), flip, top)
        lower = chosen(place == 0, top, bottom)
        x_ref[row, :] = chosen(low, upper, lower)
        y_ref[row, :] = chosen(low, lower, upper)


def arrive_far_kernel(count, place_ref, x_ref, y_ref, y_in_ref, x_in_ref, *refs):
    before_refs, after_refs, band_ref = refs[:2], refs[2:4], refs[4]
    place = place_ref[0, 0]
    low = place % 4 < 2
    start_end, last_end = place == 0, place == count - 1

    def read_before(start):
        row = pl.ds(start, CHUNK)
        x, y, x_in, y_in = x_ref[row, :], y_ref[row, :], x_in_ref[row, :], y_in_ref[row, :]
        top = chosen(start_end, y, chosen(low, y_in, x_in))
        bottom = chosen(start_end, y_in, chosen(low, y, x))
        before_refs[0][row, :] = top
        before_refs[1][row, :] = bottom
        return top, bottom

    def read_after(start):
        row = pl.ds(start, CHUNK)
        x, y, x_in, y_in = x_ref[row, :], y_ref[row, :], x_in_ref[row, :], y_in_ref[row, :]
        top = chosen(low, x, chosen(last_end, y_in, y))
        bottom = chosen(low, x_in, chosen(last_end, y, y_in))
        after_refs[0][row, :] = top
        after_refs[1][row, :] = bottom
        return top, bottom

    rows = x_ref.shape[0]
    band_ref[:PACKED_ROWS, :] = bands_of(read_before, rows)
    band_ref[PACKED_ROWS:, :] = bands_of(read_after, rows)


def finish_kernel(
    count, place_ref, top_before_ref, bottom_before_ref, top_after_ref, bottom_after_ref, parts_ref, out_ref
):
    place = place_ref[0, 0]
    packed = ordered_sum(parts_ref)
    angles_before = wide(three_angles(packed[:PACKED_ROWS]))
    angles_after = wide(three_angles(packed[PACKED_ROWS:]))
    for row in chunks(out_ref):
        top, bottom = rotated(top_before_ref[row, :], bottom_before_ref[row, :], angles_before)
        out_ref[row, :HALF] = chosen(place == 1, reverse(bottom), top)
        top, bottom = rotated(top_after_ref[row, :], bottom_after_ref[row, :], angles_after)
        out_ref[row, HALF:] = chosen(place == count - 1, top, reverse(bottom))


def call(kernel, inputs, outputs, scalars=0):
    spec = pl.BlockSpec(memory_space=pltpu.VMEM)
    return pl.pallas_call(
        kernel,
        in_specs=[pl.BlockSpec(memory_space=pltpu.SMEM)] * scalars + [spec] * (len(inputs) - scalars),
        out_specs=[spec] * len(outputs),
        out_shape=[jax.ShapeDtypeStruct(shape, jnp.float32) for shape in outputs],
        compiler_params=pltpu.CompilerParams(vmem_limit_bytes=8 * 1024 * 1024),
    )(*inputs)


def from_all(x, axes):
    count = lax.axis_size(axes)
    copies = jnp.broadcast_to(x[None], (count, *x.shape))
    return lax.all_to_all(copies, axes, 0, 0, tiled=True)


def row_parts(x):
    return from_all(ordered_sum(from_all(x, ("half", "near"))), "far")


def exchange(x, edges):
    return lax.ppermute(x, "pair", edges + [(j, i) for i, j in edges])


def per_device(snapshots):
    rows = snapshots.shape[0]
    count = lax.axis_size("pair")
    place = lax.axis_index("pair").astype(jnp.int32).reshape(1, 1)
    block, packed = (rows, HALF), (PACKED_ROWS, LANES)
    line = list(range(count))
    odd_edges, even_edges = list(zip(line[1:-1:2], line[2::2])), list(zip(line[::2], line[1::2]))
    cycle = line[::2] + line[::-2]
    x_edges = list(zip(cycle[::2], cycle[1::2]))
    y_edges = list(zip(cycle[1::2], cycle[2::2] + cycle[:1]))

    top, bottom, band = call(start_kernel, [snapshots], [block, block, packed])
    kept, odd, even = call(
        rotate_kernel, [place, top, bottom, row_parts(band)], [block] * 3, 1
    )
    top, bottom, band = call(
        functools.partial(arrive_kernel, count),
        [place, kept, exchange(odd, odd_edges), exchange(even, even_edges)],
        [block, block, packed],
        1,
    )
    x, y = call(
        functools.partial(rotate_far_kernel, count),
        [place, top, bottom, row_parts(band)],
        [block] * 2,
        1,
    )
    y_in = exchange(y, y_edges)
    x_in = exchange(x, x_edges)
    *blocks, band = call(
        functools.partial(arrive_far_kernel, count),
        [place, x, y, y_in, x_in],
        [block] * 4 + [(2 * PACKED_ROWS, LANES)],
        1,
    )
    (out,) = call(
        functools.partial(finish_kernel, count),
        [place, *blocks, row_parts(band)],
        [(rows, 2 * HALF)],
        1,
    )
    return out


def solution(mesh):
    pairs, rows = mesh.devices.shape
    fine = Mesh(mesh.devices.reshape(pairs, 2, rows // 4, 2), ("pair", "half", "far", "near"))
    spec = P(("half", "far", "near"), "pair")
    return jax.shard_map(
        per_device, mesh=fine, in_specs=(spec,), out_specs=spec, check_vma=False
    )
```

```python
import functools

import jax
import jax.numpy as jnp
from jax import lax
from jax.experimental import pallas as pl
from jax.experimental.pallas import tpu as pltpu
from jax.sharding import Mesh, PartitionSpec as P

HALF = 256
LANES = 128
BANDS = 11
PACKED_ROWS = 24
CHUNK = 8


def lanes_of(x):
    return lax.broadcasted_iota(jnp.int32, x.shape, 1)


def roll(x, by):
    return pltpu.roll(x, by % HALF, 1)


def halves(x):
    return x[:, :LANES], x[:, LANES:]


def reverse(x):
    left, right = halves(x)
    return jnp.concatenate([right, left], axis=1)


def split(top, bottom):
    (top_left, top_right), (bottom_left, bottom_right) = halves(top), halves(bottom)
    ahead = jnp.concatenate([top_left, bottom_right], axis=1)
    back = jnp.concatenate([bottom_left, top_right], axis=1)
    return ahead, back


def pick(x, index):
    return jnp.take_along_axis(x, index, axis=1)


def to_cycle(x):
    left, right = halves(x)
    lane = lanes_of(left)
    up, down = 2 * lane % LANES, (2 * LANES - 1 - 2 * lane) % LANES
    first = lane < LANES // 2
    return jnp.concatenate(
        [
            jnp.where(first, pick(left, up), pick(right, up)),
            jnp.where(first, pick(right, down), pick(left, down)),
        ],
        axis=1,
    )


def from_cycle(x):
    left, right = halves(x)
    lane = lanes_of(left)
    half = lane // 2
    even = lane % 2 == 0
    low = jnp.where(even, pick(left, half), pick(right, LANES - 1 - half))
    high = jnp.where(even, pick(left, LANES // 2 + half), pick(right, LANES // 2 - 1 - half))
    return jnp.concatenate([low, high], axis=1)


def turn(ahead, back, matrix):
    m00, m01, m10, m11 = matrix
    return m00 * ahead + m01 * back, m10 * ahead + m11 * back


def swap_at(lane, ahead, back):
    here = lanes_of(ahead) == lane
    return jnp.where(here, back, ahead), jnp.where(here, ahead, back)


def band_products(top, bottom):
    f, b = split(top, bottom)
    f1, b1, f2, b2 = roll(f, -1), roll(b, -1), roll(f, -2), roll(b, -2)
    return f * f, b * b, f * b, f * f1, f * b1, b * f1, b * b1, f * f2, f * b2, b * f2, b * b2


def bands_of(read, rows):
    total = None
    for start in range(0, rows, CHUNK):
        terms = band_products(*read(start))
        total = terms if total is None else [t + u for t, u in zip(total, terms)]
    return [jnp.sum(t, axis=0, keepdims=True) for t in total]


def pack(*pair_bands):
    left = [bands[k][:, :LANES] for k in range(BANDS) for bands in pair_bands]
    right = [bands[k][:, LANES:] for k in range(BANDS) for bands in pair_bands]
    blank = jnp.zeros((len(pair_bands) * (PACKED_ROWS - 2 * BANDS), LANES), jnp.float32)
    return jnp.concatenate(left + right + [blank], axis=0)


def unpack(packed):
    count = packed.shape[0] // PACKED_ROWS
    rows = [packed[k * count : (k + 1) * count] for k in range(2 * BANDS)]
    return [jnp.concatenate([rows[k], rows[BANDS + k]], axis=1) for k in range(BANDS)]


def matrix_of(ff, bb, fb, upper_ahead, swapped_lane):
    a, b, c = jnp.where(upper_ahead, ff, bb), jnp.where(upper_ahead, bb, ff), fb
    difference = b - a
    sign = jnp.where(difference >= 0, 1.0, -1.0)
    radius = jnp.sqrt(difference * difference + 4.0 * c * c + (1e-06 * (a + b)) ** 2)
    tangent = 2.0 * c * sign / (jnp.abs(difference) + radius)
    cosine = 1.0 / jnp.sqrt(1.0 + tangent * tangent)
    sine = tangent * cosine
    sine = jnp.where(upper_ahead, sine, -sine)
    if swapped_lane is None:
        return cosine, -sine, sine, cosine
    here = lanes_of(ff) == swapped_lane
    rows = jnp.where(here, sine, cosine), jnp.where(here, cosine, sine)
    return rows[0], jnp.where(here, cosine, -sine), rows[1], jnp.where(here, -sine, cosine)


def turn_diagonal(ff, bb, fb, matrix):
    m00, m01, m10, m11 = matrix
    return (
        m00 * m00 * ff + 2.0 * m00 * m01 * fb + m01 * m01 * bb,
        m10 * m10 * ff + 2.0 * m10 * m11 * fb + m11 * m11 * bb,
        m00 * m10 * ff + (m00 * m11 + m01 * m10) * fb + m01 * m11 * bb,
    )


def turn_block(block, left, right):
    ff, fb, bf, bb = block
    ff, bf = turn(ff, bf, left)
    fb, bb = turn(fb, bb, left)
    ff, fb = turn(ff, fb, right)
    bf, bb = turn(bf, bb, right)
    return ff, fb, bf, bb


def shifted(matrix, by):
    return [roll(m, -by) for m in matrix]


def three_matrices(packed):
    rows = unpack(packed)
    lane = lanes_of(rows[0])
    left = lane < LANES
    first = matrix_of(*rows[:3], left, 0)
    ff, bb, fb = turn_diagonal(*rows[:3], first)
    near_ff, near_fb, _, near_bb = turn_block(rows[3:7], first, shifted(first, 1))
    _, far_fb, _, _ = turn_block(rows[7:11], first, shifted(first, 2))
    diagonal = ff, roll(bb, -1), near_fb
    second = matrix_of(*diagonal, left, HALF - 1)
    block = near_ff, far_fb, roll(fb, -1), roll(near_bb, -1)
    ff, bb, _ = turn_diagonal(*diagonal, second)
    _, cross, _, _ = turn_block(block, second, shifted(second, 1))
    upper_ahead = (lane < LANES - 1) | (lane == HALF - 1)
    return first, second, matrix_of(ff, roll(bb, -1), cross, upper_ahead, None)


def ordered_sum(x):
    return functools.reduce(jnp.add, [x[i] for i in range(x.shape[0])])


def chosen(condition, x, y):
    return jnp.where(condition, x, y)


def wide(matrices, index=0):
    row = slice(index, index + 1)
    return [[jnp.broadcast_to(v[row], (CHUNK, HALF)) for v in matrix] for matrix in matrices]


def rotated(top, bottom, matrices):
    first, second, third = matrices
    ahead, back = turn(*split(top, bottom), first)
    ahead, back = turn(ahead, roll(back, -1), second)
    ahead, back = turn(ahead, roll(back, -1), third)
    ahead, back = swap_at(HALF - 1, ahead, roll(back, 1))
    return split(*swap_at(0, ahead, roll(back, 1)))


def chunks(ref):
    return [pl.ds(start, CHUNK) for start in range(0, ref.shape[0], CHUNK)]


def start_kernel(work_ref, top_ref, bottom_ref, band_ref):
    def read(start):
        row = pl.ds(start, CHUNK)
        top = to_cycle(work_ref[row, :HALF])
        bottom = reverse(to_cycle(work_ref[row, HALF:]))
        top_ref[row, :] = top
        bottom_ref[row, :] = bottom
        return top, bottom

    band_ref[...] = pack(bands_of(read, work_ref.shape[0]))


def rotate_kernel(place_ref, top_ref, bottom_ref, parts_ref, kept_ref, odd_ref, even_ref):
    place = place_ref[0, 0]
    at_odd = place % 2 == 1
    matrices = wide(three_matrices(ordered_sum(parts_ref)))
    for row in chunks(top_ref):
        top, bottom = rotated(top_ref[row, :], bottom_ref[row, :], matrices)
        right = chosen(place == 0, reverse(bottom), top)
        kept_ref[row, :] = chosen(place == 0, top, reverse(top))
        odd_ref[row, :] = chosen(at_odd, right, bottom)
        even_ref[row, :] = chosen(at_odd, bottom, right)


def arrive_kernel(count, place_ref, kept_ref, odd_ref, even_ref, top_ref, bottom_ref, band_ref):
    place = place_ref[0, 0]
    at_odd = place % 2 == 1

    def read(start):
        row = pl.ds(start, CHUNK)
        kept, odd, even = kept_ref[row, :], odd_ref[row, :], even_ref[row, :]
        top = chosen(place == 0, kept, chosen(at_odd, even, odd))
        bottom = chosen(place == count - 1, kept, chosen(at_odd, odd, even))
        top_ref[row, :] = top
        bottom_ref[row, :] = bottom
        return top, bottom

    band_ref[...] = pack(bands_of(read, kept_ref.shape[0]))


def rotate_far_kernel(count, place_ref, top_ref, bottom_ref, parts_ref, y_ref, x_ref):
    place = place_ref[0, 0]
    low = place % 4 < 2
    matrices = wide(three_matrices(ordered_sum(parts_ref)))
    for row in chunks(top_ref):
        top, bottom = rotated(top_ref[row, :], bottom_ref[row, :], matrices)
        flip = reverse(chosen(place == 0, bottom, top))
        upper = chosen((place == 0) | (place == count - 1), flip, top)
        lower = chosen(place == 0, top, bottom)
        x_ref[row, :] = chosen(low, upper, lower)
        y_ref[row, :] = chosen(low, lower, upper)


def arrive_far_kernel(count, place_ref, y_ref, x_ref, y_in_ref, x_in_ref, *refs):
    before_refs, after_refs, band_ref = refs[:2], refs[2:4], refs[4]
    place = place_ref[0, 0]
    low = place % 4 < 2
    start_end, last_end = place == 0, place == count - 1

    def read_before(start):
        row = pl.ds(start, CHUNK)
        x, y, x_in, y_in = x_ref[row, :], y_ref[row, :], x_in_ref[row, :], y_in_ref[row, :]
        top = chosen(start_end, y, chosen(low, y_in, x_in))
        bottom = chosen(start_end, y_in, chosen(low, y, x))
        before_refs[0][row, :] = top
        before_refs[1][row, :] = bottom
        return top, bottom

    def read_after(start):
        row = pl.ds(start, CHUNK)
        x, y, x_in, y_in = x_ref[row, :], y_ref[row, :], x_in_ref[row, :], y_in_ref[row, :]
        top = chosen(low, x, chosen(last_end, y_in, y))
        bottom = chosen(low, x_in, chosen(last_end, y, y_in))
        after_refs[0][row, :] = top
        after_refs[1][row, :] = bottom
        return top, bottom

    rows = x_ref.shape[0]
    band_ref[...] = pack(bands_of(read_before, rows), bands_of(read_after, rows))


def finish_kernel(
    count, place_ref, top_before_ref, bottom_before_ref, top_after_ref, bottom_after_ref, parts_ref, out_ref
):
    place = place_ref[0, 0]
    both = three_matrices(ordered_sum(parts_ref))
    matrices_before, matrices_after = wide(both, 0), wide(both, 1)
    for row in chunks(out_ref):
        top, bottom = rotated(top_before_ref[row, :], bottom_before_ref[row, :], matrices_before)
        out_ref[row, :HALF] = from_cycle(chosen(place == 1, reverse(bottom), top))
        top, bottom = rotated(top_after_ref[row, :], bottom_after_ref[row, :], matrices_after)
        out_ref[row, HALF:] = from_cycle(chosen(place == count - 1, top, reverse(bottom)))


def call(kernel, inputs, outputs, scalars=0):
    spec = pl.BlockSpec(memory_space=pltpu.VMEM)
    return pl.pallas_call(
        kernel,
        in_specs=[pl.BlockSpec(memory_space=pltpu.SMEM)] * scalars + [spec] * (len(inputs) - scalars),
        out_specs=[spec] * len(outputs),
        out_shape=[jax.ShapeDtypeStruct(shape, jnp.float32) for shape in outputs],
        compiler_params=pltpu.CompilerParams(vmem_limit_bytes=8 * 1024 * 1024),
    )(*inputs)


def from_all(x, axes):
    count = lax.axis_size(axes)
    copies = jnp.broadcast_to(x[None], (count, *x.shape))
    return lax.all_to_all(copies, axes, 0, 0, tiled=True)


def row_parts(x):
    return from_all(ordered_sum(from_all(x, ("half", "near"))), "far")


def exchange(x, edges):
    return lax.ppermute(x, "pair", edges + [(j, i) for i, j in edges])


def per_device(snapshots):
    rows = snapshots.shape[0]
    count = lax.axis_size("pair")
    place = lax.axis_index("pair").astype(jnp.int32).reshape(1, 1)
    block, packed = (rows, HALF), (PACKED_ROWS, LANES)
    line = list(range(count))
    odd_edges, even_edges = list(zip(line[1:-1:2], line[2::2])), list(zip(line[::2], line[1::2]))
    cycle = line[::2] + line[::-2]
    x_edges = list(zip(cycle[::2], cycle[1::2]))
    y_edges = list(zip(cycle[1::2], cycle[2::2] + cycle[:1]))

    top, bottom, band = call(start_kernel, [snapshots], [block, block, packed])
    kept, odd, even = call(
        rotate_kernel, [place, top, bottom, row_parts(band)], [block] * 3, 1
    )
    top, bottom, band = call(
        functools.partial(arrive_kernel, count),
        [place, kept, exchange(odd, odd_edges), exchange(even, even_edges)],
        [block, block, packed],
        1,
    )
    y, x = call(
        functools.partial(rotate_far_kernel, count),
        [place, top, bottom, row_parts(band)],
        [block] * 2,
        1,
    )
    y_in = exchange(y, y_edges)
    x_in = exchange(x, x_edges)
    *blocks, band = call(
        functools.partial(arrive_far_kernel, count),
        [place, y, x, y_in, x_in],
        [block] * 4 + [(2 * PACKED_ROWS, LANES)],
        1,
    )
    (out,) = call(
        functools.partial(finish_kernel, count),
        [place, *blocks, row_parts(band)],
        [(rows, 2 * HALF)],
        1,
    )
    return out


def solution(mesh):
    pairs, rows = mesh.devices.shape
    fine = Mesh(mesh.devices.reshape(pairs, 2, rows // 4, 2), ("pair", "half", "far", "near"))
    spec = P(("half", "far", "near"), "pair")
    return jax.shard_map(
        per_device, mesh=fine, in_specs=(spec,), out_specs=spec, check_vma=False
    )
```

```python
import functools

import jax
import jax.numpy as jnp
from jax import lax
from jax.experimental import pallas as pl
from jax.experimental.pallas import tpu as pltpu
from jax.sharding import Mesh, PartitionSpec as P

HALF = 256
LANES = 128
BANDS = 11
PACKED_ROWS = 24
CHUNK = 8


def lanes_of(x):
    return lax.broadcasted_iota(jnp.int32, x.shape, 1)


def roll(x, by):
    return pltpu.roll(x, by % HALF, 1)


def halves(x):
    return x[:, :LANES], x[:, LANES:]


def reverse(x):
    left, right = halves(x)
    return jnp.concatenate([right, left], axis=1)


def split(top, bottom):
    (top_left, top_right), (bottom_left, bottom_right) = halves(top), halves(bottom)
    ahead = jnp.concatenate([top_left, bottom_right], axis=1)
    back = jnp.concatenate([bottom_left, top_right], axis=1)
    return ahead, back


def pick(x, index):
    return jnp.take_along_axis(x, index, axis=1)


def to_cycle(x):
    left, right = halves(x)
    lane = lanes_of(left)
    up, down = 2 * lane % LANES, (2 * LANES - 1 - 2 * lane) % LANES
    first = lane < LANES // 2
    return jnp.concatenate(
        [
            jnp.where(first, pick(left, up), pick(right, up)),
            jnp.where(first, pick(right, down), pick(left, down)),
        ],
        axis=1,
    )


def from_cycle(x):
    left, right = halves(x)
    lane = lanes_of(left)
    half = lane // 2
    even = lane % 2 == 0
    low = jnp.where(even, pick(left, half), pick(right, LANES - 1 - half))
    high = jnp.where(even, pick(left, LANES // 2 + half), pick(right, LANES // 2 - 1 - half))
    return jnp.concatenate([low, high], axis=1)


def turn(ahead, back, matrix):
    m00, m01, m10, m11 = matrix
    return m00 * ahead + m01 * back, m10 * ahead + m11 * back


def swap_at(lane, ahead, back):
    here = lanes_of(ahead) == lane
    return jnp.where(here, back, ahead), jnp.where(here, ahead, back)


def band_products(top, bottom):
    f, b = split(top, bottom)
    f1, b1, f2, b2 = roll(f, -1), roll(b, -1), roll(f, -2), roll(b, -2)
    return f * f, b * b, f * b, f * f1, f * b1, b * f1, b * b1, f * f2, f * b2, b * f2, b * b2


def bands_of(read, rows):
    total = None
    for start in range(0, rows, CHUNK):
        terms = band_products(*read(start))
        total = terms if total is None else [t + u for t, u in zip(total, terms)]
    return [jnp.sum(t, axis=0, keepdims=True) for t in total]


def pack(*pair_bands):
    left = [bands[k][:, :LANES] for k in range(BANDS) for bands in pair_bands]
    right = [bands[k][:, LANES:] for k in range(BANDS) for bands in pair_bands]
    blank = jnp.zeros((len(pair_bands) * (PACKED_ROWS - 2 * BANDS), LANES), jnp.float32)
    return jnp.concatenate(left + right + [blank], axis=0)


def unpack(packed):
    count = packed.shape[0] // PACKED_ROWS
    rows = [packed[k * count : (k + 1) * count] for k in range(2 * BANDS)]
    return [jnp.concatenate([rows[k], rows[BANDS + k]], axis=1) for k in range(BANDS)]


def matrix_of(ff, bb, fb, upper_ahead, swapped_lane):
    a, b, c = jnp.where(upper_ahead, ff, bb), jnp.where(upper_ahead, bb, ff), fb
    difference = b - a
    sign = jnp.where(difference >= 0, 1.0, -1.0)
    radius = jnp.sqrt(difference * difference + 4.0 * c * c + (1e-06 * (a + b)) ** 2)
    tangent = 2.0 * c * sign / (jnp.abs(difference) + radius)
    cosine = 1.0 / jnp.sqrt(1.0 + tangent * tangent)
    sine = tangent * cosine
    sine = jnp.where(upper_ahead, sine, -sine)
    if swapped_lane is None:
        return cosine, -sine, sine, cosine
    here = lanes_of(ff) == swapped_lane
    rows = jnp.where(here, sine, cosine), jnp.where(here, cosine, sine)
    return rows[0], jnp.where(here, cosine, -sine), rows[1], jnp.where(here, -sine, cosine)


def turn_diagonal(ff, bb, fb, matrix):
    m00, m01, m10, m11 = matrix
    return (
        m00 * m00 * ff + 2.0 * m00 * m01 * fb + m01 * m01 * bb,
        m10 * m10 * ff + 2.0 * m10 * m11 * fb + m11 * m11 * bb,
        m00 * m10 * ff + (m00 * m11 + m01 * m10) * fb + m01 * m11 * bb,
    )


def turn_block(block, left, right):
    ff, fb, bf, bb = block
    ff, bf = turn(ff, bf, left)
    fb, bb = turn(fb, bb, left)
    ff, fb = turn(ff, fb, right)
    bf, bb = turn(bf, bb, right)
    return ff, fb, bf, bb


def shifted(matrix, by):
    return [roll(m, -by) for m in matrix]


def three_matrices(packed):
    rows = unpack(packed)
    lane = lanes_of(rows[0])
    left = lane < LANES
    first = matrix_of(*rows[:3], left, 0)
    ff, bb, fb = turn_diagonal(*rows[:3], first)
    near_ff, near_fb, _, near_bb = turn_block(rows[3:7], first, shifted(first, 1))
    _, far_fb, _, _ = turn_block(rows[7:11], first, shifted(first, 2))
    diagonal = ff, roll(bb, -1), near_fb
    second = matrix_of(*diagonal, left, HALF - 1)
    block = near_ff, far_fb, roll(fb, -1), roll(near_bb, -1)
    ff, bb, _ = turn_diagonal(*diagonal, second)
    _, cross, _, _ = turn_block(block, second, shifted(second, 1))
    upper_ahead = (lane < LANES - 1) | (lane == HALF - 1)
    return first, second, matrix_of(ff, roll(bb, -1), cross, upper_ahead, None)


def ordered_sum(x):
    return functools.reduce(jnp.add, [x[i] for i in range(x.shape[0])])


def chosen(condition, x, y):
    return jnp.where(condition, x, y)


def wide(matrices, index=0):
    row = slice(index, index + 1)
    return [[jnp.broadcast_to(v[row], (CHUNK, HALF)) for v in matrix] for matrix in matrices]


def rotated(top, bottom, matrices):
    first, second, third = matrices
    ahead, back = turn(*split(top, bottom), first)
    ahead, back = turn(ahead, roll(back, -1), second)
    ahead, back = turn(ahead, roll(back, -1), third)
    ahead, back = swap_at(HALF - 1, ahead, roll(back, 1))
    return split(*swap_at(0, ahead, roll(back, 1)))


def chunks(ref):
    return [pl.ds(start, CHUNK) for start in range(0, ref.shape[0], CHUNK)]


def start_kernel(work_ref, top_ref, bottom_ref, band_ref):
    def read(start):
        row = pl.ds(start, CHUNK)
        top = to_cycle(work_ref[row, :HALF])
        bottom = reverse(to_cycle(work_ref[row, HALF:]))
        top_ref[row, :] = top
        bottom_ref[row, :] = bottom
        return top, bottom

    band_ref[...] = pack(bands_of(read, work_ref.shape[0]))


def rotate_kernel(place_ref, top_ref, bottom_ref, parts_ref, kept_ref, odd_ref, even_ref):
    place = place_ref[0, 0]
    at_odd = place % 2 == 1
    matrices = wide(three_matrices(ordered_sum(parts_ref)))
    for row in chunks(top_ref):
        top, bottom = rotated(top_ref[row, :], bottom_ref[row, :], matrices)
        right = chosen(place == 0, reverse(bottom), top)
        kept_ref[row, :] = chosen(place == 0, top, reverse(top))
        odd_ref[row, :] = chosen(at_odd, right, bottom)
        even_ref[row, :] = chosen(at_odd, bottom, right)


def arrive_kernel(count, place_ref, kept_ref, odd_ref, even_ref, top_ref, bottom_ref, band_ref):
    place = place_ref[0, 0]
    at_odd = place % 2 == 1

    def read(start):
        row = pl.ds(start, CHUNK)
        kept, odd, even = kept_ref[row, :], odd_ref[row, :], even_ref[row, :]
        top = chosen(place == 0, kept, chosen(at_odd, even, odd))
        bottom = chosen(place == count - 1, kept, chosen(at_odd, odd, even))
        top_ref[row, :] = top
        bottom_ref[row, :] = bottom
        return top, bottom

    band_ref[...] = pack(bands_of(read, kept_ref.shape[0]))


def rotate_far_kernel(count, place_ref, top_ref, bottom_ref, parts_ref, y_ref, x_ref):
    place = place_ref[0, 0]
    low = place % 4 < 2
    matrices = wide(three_matrices(ordered_sum(parts_ref)))
    for row in chunks(top_ref):
        top, bottom = rotated(top_ref[row, :], bottom_ref[row, :], matrices)
        flip = reverse(chosen(place == 0, bottom, top))
        upper = chosen((place == 0) | (place == count - 1), flip, top)
        lower = chosen(place == 0, top, bottom)
        x_ref[row, :] = chosen(low, upper, lower)
        y_ref[row, :] = chosen(low, lower, upper)


def arrive_far_kernel(count, place_ref, y_ref, x_ref, y_in_ref, x_in_ref, *refs):
    before_refs, after_refs, band_ref = refs[:2], refs[2:4], refs[4]
    place = place_ref[0, 0]
    low = place % 4 < 2
    start_end, last_end = place == 0, place == count - 1

    def read_before(start):
        row = pl.ds(start, CHUNK)
        x, y, x_in, y_in = x_ref[row, :], y_ref[row, :], x_in_ref[row, :], y_in_ref[row, :]
        top = chosen(start_end, y, chosen(low, y_in, x_in))
        bottom = chosen(start_end, y_in, chosen(low, y, x))
        before_refs[0][row, :] = top
        before_refs[1][row, :] = bottom
        return top, bottom

    def read_after(start):
        row = pl.ds(start, CHUNK)
        x, y, x_in, y_in = x_ref[row, :], y_ref[row, :], x_in_ref[row, :], y_in_ref[row, :]
        top = chosen(low, x, chosen(last_end, y_in, y))
        bottom = chosen(low, x_in, chosen(last_end, y, y_in))
        after_refs[0][row, :] = top
        after_refs[1][row, :] = bottom
        return top, bottom

    rows = x_ref.shape[0]
    band_ref[...] = pack(bands_of(read_before, rows), bands_of(read_after, rows))


def finish_kernel(
    count, place_ref, top_before_ref, bottom_before_ref, top_after_ref, bottom_after_ref, parts_ref, out_ref
):
    place = place_ref[0, 0]
    both = three_matrices(ordered_sum(parts_ref))
    matrices_before, matrices_after = wide(both, 0), wide(both, 1)
    for row in chunks(out_ref):
        top, bottom = rotated(top_before_ref[row, :], bottom_before_ref[row, :], matrices_before)
        out_ref[row, :HALF] = from_cycle(chosen(place == 1, reverse(bottom), top))
        top, bottom = rotated(top_after_ref[row, :], bottom_after_ref[row, :], matrices_after)
        out_ref[row, HALF:] = from_cycle(chosen(place == count - 1, top, reverse(bottom)))


def call(kernel, inputs, outputs, scalars=0):
    spec = pl.BlockSpec(memory_space=pltpu.VMEM)
    return pl.pallas_call(
        kernel,
        in_specs=[pl.BlockSpec(memory_space=pltpu.SMEM)] * scalars + [spec] * (len(inputs) - scalars),
        out_specs=[spec] * len(outputs),
        out_shape=[jax.ShapeDtypeStruct(shape, jnp.float32) for shape in outputs],
        compiler_params=pltpu.CompilerParams(vmem_limit_bytes=8 * 1024 * 1024),
    )(*inputs)


def from_all(x, axes, first=0):
    count = lax.axis_size(axes)
    copies = jnp.broadcast_to(x[None], (count, *x.shape))
    order = [(first + i) % count for i in range(count)]
    groups = [order] if first else None
    return lax.all_to_all(copies, axes, 0, 0, tiled=True, axis_index_groups=groups)


def row_parts(x):
    near = ordered_sum(from_all(x, ("half", "near")))
    return from_all(near, "far", lax.axis_size("far") // 2)


def exchange(x, edges):
    return lax.ppermute(x, "pair", edges + [(j, i) for i, j in edges])


def per_device(snapshots):
    rows = snapshots.shape[0]
    count = lax.axis_size("pair")
    place = lax.axis_index("pair").astype(jnp.int32).reshape(1, 1)
    block, packed = (rows, HALF), (PACKED_ROWS, LANES)
    line = list(range(count))
    odd_edges, even_edges = list(zip(line[1:-1:2], line[2::2])), list(zip(line[::2], line[1::2]))
    cycle = line[::2] + line[::-2]
    x_edges = list(zip(cycle[::2], cycle[1::2]))
    y_edges = list(zip(cycle[1::2], cycle[2::2] + cycle[:1]))

    top, bottom, band = call(start_kernel, [snapshots], [block, block, packed])
    kept, odd, even = call(
        rotate_kernel, [place, top, bottom, row_parts(band)], [block] * 3, 1
    )
    top, bottom, band = call(
        functools.partial(arrive_kernel, count),
        [place, kept, exchange(odd, odd_edges), exchange(even, even_edges)],
        [block, block, packed],
        1,
    )
    y, x = call(
        functools.partial(rotate_far_kernel, count),
        [place, top, bottom, row_parts(band)],
        [block] * 2,
        1,
    )
    y_in = exchange(y, y_edges)
    x_in = exchange(x, x_edges)
    *blocks, band = call(
        functools.partial(arrive_far_kernel, count),
        [place, y, x, y_in, x_in],
        [block] * 4 + [(2 * PACKED_ROWS, LANES)],
        1,
    )
    (out,) = call(
        functools.partial(finish_kernel, count),
        [place, *blocks, row_parts(band)],
        [(rows, 2 * HALF)],
        1,
    )
    return out


def solution(mesh):
    pairs, rows = mesh.devices.shape
    fine = Mesh(mesh.devices.reshape(pairs, 2, rows // 4, 2), ("pair", "half", "far", "near"))
    spec = P(("half", "far", "near"), "pair")
    return jax.shard_map(
        per_device, mesh=fine, in_specs=(spec,), out_specs=spec, check_vma=False
    )
```

```python
import functools

import jax
import jax.numpy as jnp
from jax import lax
from jax.experimental import pallas as pl
from jax.experimental.pallas import tpu as pltpu
from jax.sharding import Mesh, PartitionSpec as P

HALF = 256
LANES = 128
BANDS = 11
PACKED_ROWS = 24
CHUNK = 8


def lanes_of(x):
    return lax.broadcasted_iota(jnp.int32, x.shape, 1)


def roll(x, by):
    return pltpu.roll(x, by % HALF, 1)


def halves(x):
    return x[:, :LANES], x[:, LANES:]


def reverse(x):
    left, right = halves(x)
    return jnp.concatenate([right, left], axis=1)


def split(top, bottom):
    (top_left, top_right), (bottom_left, bottom_right) = halves(top), halves(bottom)
    ahead = jnp.concatenate([top_left, bottom_right], axis=1)
    back = jnp.concatenate([bottom_left, top_right], axis=1)
    return ahead, back


def pick(x, index):
    return jnp.take_along_axis(x, index, axis=1)


def to_cycle(x):
    left, right = halves(x)
    lane = lanes_of(left)
    up, down = 2 * lane % LANES, (2 * LANES - 1 - 2 * lane) % LANES
    first = lane < LANES // 2
    return jnp.concatenate(
        [
            jnp.where(first, pick(left, up), pick(right, up)),
            jnp.where(first, pick(right, down), pick(left, down)),
        ],
        axis=1,
    )


def from_cycle(x):
    left, right = halves(x)
    lane = lanes_of(left)
    half = lane // 2
    even = lane % 2 == 0
    low = jnp.where(even, pick(left, half), pick(right, LANES - 1 - half))
    high = jnp.where(even, pick(left, LANES // 2 + half), pick(right, LANES // 2 - 1 - half))
    return jnp.concatenate([low, high], axis=1)


def turn(ahead, back, matrix):
    m00, m01, m10, m11 = matrix
    return m00 * ahead + m01 * back, m10 * ahead + m11 * back


def swap_at(lane, ahead, back):
    here = lanes_of(ahead) == lane
    return jnp.where(here, back, ahead), jnp.where(here, ahead, back)


def band_products(top, bottom):
    f, b = split(top, bottom)
    f1, b1, f2, b2 = roll(f, -1), roll(b, -1), roll(f, -2), roll(b, -2)
    return f * f, b * b, f * b, f * f1, f * b1, b * f1, b * b1, f * f2, f * b2, b * f2, b * b2


def bands_of(read, rows):
    total = None
    for start in range(0, rows, CHUNK):
        terms = band_products(*read(start))
        total = terms if total is None else [t + u for t, u in zip(total, terms)]
    return [jnp.sum(t, axis=0, keepdims=True) for t in total]


def pack(*pair_bands):
    left = [bands[k][:, :LANES] for k in range(BANDS) for bands in pair_bands]
    right = [bands[k][:, LANES:] for k in range(BANDS) for bands in pair_bands]
    blank = jnp.zeros((len(pair_bands) * (PACKED_ROWS - 2 * BANDS), LANES), jnp.float32)
    return jnp.concatenate(left + right + [blank], axis=0)


def unpack(packed):
    count = packed.shape[0] // PACKED_ROWS
    rows = [packed[k * count : (k + 1) * count] for k in range(2 * BANDS)]
    return [jnp.concatenate([rows[k], rows[BANDS + k]], axis=1) for k in range(BANDS)]


def matrix_of(ff, bb, fb, upper_ahead, swapped_lane):
    a, b, c = jnp.where(upper_ahead, ff, bb), jnp.where(upper_ahead, bb, ff), fb
    difference = b - a
    sign = jnp.where(difference >= 0, 1.0, -1.0)
    radius = jnp.sqrt(difference * difference + 4.0 * c * c + (1e-06 * (a + b)) ** 2)
    tangent = 2.0 * c * sign / (jnp.abs(difference) + radius)
    cosine = 1.0 / jnp.sqrt(1.0 + tangent * tangent)
    sine = tangent * cosine
    sine = jnp.where(upper_ahead, sine, -sine)
    if swapped_lane is None:
        return cosine, -sine, sine, cosine
    here = lanes_of(ff) == swapped_lane
    rows = jnp.where(here, sine, cosine), jnp.where(here, cosine, sine)
    return rows[0], jnp.where(here, cosine, -sine), rows[1], jnp.where(here, -sine, cosine)


def turn_diagonal(ff, bb, fb, matrix):
    m00, m01, m10, m11 = matrix
    return (
        m00 * m00 * ff + 2.0 * m00 * m01 * fb + m01 * m01 * bb,
        m10 * m10 * ff + 2.0 * m10 * m11 * fb + m11 * m11 * bb,
        m00 * m10 * ff + (m00 * m11 + m01 * m10) * fb + m01 * m11 * bb,
    )


def turn_block(block, left, right):
    ff, fb, bf, bb = block
    ff, bf = turn(ff, bf, left)
    fb, bb = turn(fb, bb, left)
    ff, fb = turn(ff, fb, right)
    bf, bb = turn(bf, bb, right)
    return ff, fb, bf, bb


def shifted(matrix, by):
    return [roll(m, -by) for m in matrix]


def three_matrices(packed):
    rows = unpack(packed)
    lane = lanes_of(rows[0])
    left = lane < LANES
    first = matrix_of(*rows[:3], left, 0)
    ff, bb, fb = turn_diagonal(*rows[:3], first)
    near_ff, near_fb, _, near_bb = turn_block(rows[3:7], first, shifted(first, 1))
    _, far_fb, _, _ = turn_block(rows[7:11], first, shifted(first, 2))
    diagonal = ff, roll(bb, -1), near_fb
    second = matrix_of(*diagonal, left, HALF - 1)
    block = near_ff, far_fb, roll(fb, -1), roll(near_bb, -1)
    ff, bb, _ = turn_diagonal(*diagonal, second)
    _, cross, _, _ = turn_block(block, second, shifted(second, 1))
    upper_ahead = (lane < LANES - 1) | (lane == HALF - 1)
    return first, second, matrix_of(ff, roll(bb, -1), cross, upper_ahead, None)


def ordered_sum(x):
    return functools.reduce(jnp.add, [x[i] for i in range(x.shape[0])])


def chosen(condition, x, y):
    return jnp.where(condition, x, y)


def wide(matrices, index=0):
    row = slice(index, index + 1)
    return [[jnp.broadcast_to(v[row], (CHUNK, HALF)) for v in matrix] for matrix in matrices]


def rotated(top, bottom, matrices):
    first, second, third = matrices
    ahead, back = turn(*split(top, bottom), first)
    ahead, back = turn(ahead, roll(back, -1), second)
    ahead, back = turn(ahead, roll(back, -1), third)
    ahead, back = swap_at(HALF - 1, ahead, roll(back, 1))
    return split(*swap_at(0, ahead, roll(back, 1)))


def chunks(ref):
    return [pl.ds(start, CHUNK) for start in range(0, ref.shape[0], CHUNK)]


def start_kernel(place_ref, work_hbm, top_ref, bottom_ref, band_ref, work_ref, sems):
    rows = work_ref.shape[0]
    size = rows // sems.shape[0]
    copies = []
    for i in range(sems.shape[0]):
        part = pl.ds(i * size, size)
        copies.append(pltpu.make_async_copy(work_hbm.at[part], work_ref.at[part], sems.at[i]))
        copies[-1].start()

    def read(start):
        if start % size == 0:
            copies[start // size].wait()
        row = pl.ds(start, CHUNK)
        top = to_cycle(work_ref[row, :HALF])
        bottom = reverse(to_cycle(work_ref[row, HALF:]))
        top_ref[row, :] = top
        bottom_ref[row, :] = bottom
        return top, bottom

    band_ref[...] = pack(bands_of(read, rows))


def rotate_kernel(place_ref, top_ref, bottom_ref, parts_ref, kept_ref, odd_ref, even_ref):
    place = place_ref[0, 0]
    at_odd = place % 2 == 1
    matrices = wide(three_matrices(ordered_sum(parts_ref)))
    for row in chunks(top_ref):
        top, bottom = rotated(top_ref[row, :], bottom_ref[row, :], matrices)
        right = chosen(place == 0, reverse(bottom), top)
        kept_ref[row, :] = chosen(place == 0, top, reverse(top))
        odd_ref[row, :] = chosen(at_odd, right, bottom)
        even_ref[row, :] = chosen(at_odd, bottom, right)


def arrive_kernel(count, place_ref, kept_ref, odd_ref, even_ref, top_ref, bottom_ref, band_ref):
    place = place_ref[0, 0]
    at_odd = place % 2 == 1

    def read(start):
        row = pl.ds(start, CHUNK)
        kept, odd, even = kept_ref[row, :], odd_ref[row, :], even_ref[row, :]
        top = chosen(place == 0, kept, chosen(at_odd, even, odd))
        bottom = chosen(place == count - 1, kept, chosen(at_odd, odd, even))
        top_ref[row, :] = top
        bottom_ref[row, :] = bottom
        return top, bottom

    band_ref[...] = pack(bands_of(read, kept_ref.shape[0]))


def rotate_far_kernel(count, place_ref, top_ref, bottom_ref, parts_ref, y_ref, x_ref):
    place = place_ref[0, 0]
    low = place % 4 < 2
    matrices = wide(three_matrices(ordered_sum(parts_ref)))
    for row in chunks(top_ref):
        top, bottom = rotated(top_ref[row, :], bottom_ref[row, :], matrices)
        flip = reverse(chosen(place == 0, bottom, top))
        upper = chosen((place == 0) | (place == count - 1), flip, top)
        lower = chosen(place == 0, top, bottom)
        x_ref[row, :] = chosen(low, upper, lower)
        y_ref[row, :] = chosen(low, lower, upper)


def arrive_far_kernel(count, place_ref, y_ref, x_ref, y_in_ref, x_in_ref, *refs):
    before_refs, after_refs, band_ref = refs[:2], refs[2:4], refs[4]
    place = place_ref[0, 0]
    low = place % 4 < 2
    start_end, last_end = place == 0, place == count - 1

    def read_before(start):
        row = pl.ds(start, CHUNK)
        x, y, x_in, y_in = x_ref[row, :], y_ref[row, :], x_in_ref[row, :], y_in_ref[row, :]
        top = chosen(start_end, y, chosen(low, y_in, x_in))
        bottom = chosen(start_end, y_in, chosen(low, y, x))
        before_refs[0][row, :] = top
        before_refs[1][row, :] = bottom
        return top, bottom

    def read_after(start):
        row = pl.ds(start, CHUNK)
        x, y, x_in, y_in = x_ref[row, :], y_ref[row, :], x_in_ref[row, :], y_in_ref[row, :]
        top = chosen(low, x, chosen(last_end, y_in, y))
        bottom = chosen(low, x_in, chosen(last_end, y, y_in))
        after_refs[0][row, :] = top
        after_refs[1][row, :] = bottom
        return top, bottom

    rows = x_ref.shape[0]
    band_ref[...] = pack(bands_of(read_before, rows), bands_of(read_after, rows))


def finish_kernel(
    count, place_ref, top_before_ref, bottom_before_ref, top_after_ref, bottom_after_ref, parts_ref, out_ref
):
    place = place_ref[0, 0]
    both = three_matrices(ordered_sum(parts_ref))
    matrices_before, matrices_after = wide(both, 0), wide(both, 1)
    for row in chunks(out_ref):
        top, bottom = rotated(top_before_ref[row, :], bottom_before_ref[row, :], matrices_before)
        out_ref[row, :HALF] = from_cycle(chosen(place == 1, reverse(bottom), top))
        top, bottom = rotated(top_after_ref[row, :], bottom_after_ref[row, :], matrices_after)
        out_ref[row, HALF:] = from_cycle(chosen(place == count - 1, top, reverse(bottom)))


def call(kernel, inputs, outputs, scratch=(), space=pltpu.VMEM):
    spec = pl.BlockSpec(memory_space=pltpu.VMEM)
    places = [pl.BlockSpec(memory_space=pltpu.SMEM)]
    return pl.pallas_call(
        kernel,
        in_specs=places + [pl.BlockSpec(memory_space=space)] * (len(inputs) - 1),
        out_specs=[spec] * len(outputs),
        out_shape=[jax.ShapeDtypeStruct(shape, jnp.float32) for shape in outputs],
        scratch_shapes=list(scratch),
        compiler_params=pltpu.CompilerParams(vmem_limit_bytes=8 * 1024 * 1024),
    )(*inputs)


def from_all(x, axes, first=0):
    count = lax.axis_size(axes)
    copies = jnp.broadcast_to(x[None], (count, *x.shape))
    order = [(first + i) % count for i in range(count)]
    groups = [order] if first else None
    return lax.all_to_all(copies, axes, 0, 0, tiled=True, axis_index_groups=groups)


def row_parts(x):
    near = ordered_sum(from_all(x, ("half", "near")))
    return from_all(near, "far", lax.axis_size("far") // 2)


def row_parts_of_ring(x):
    both = x + lax.ppermute(x, "half", [(0, 1), (1, 0)])
    ring = ("far", "near")
    return from_all(both, ring, lax.axis_size(ring) // 2)


def exchange(x, edges):
    return lax.ppermute(x, "pair", edges + [(j, i) for i, j in edges])


def per_device(snapshots):
    rows = snapshots.shape[0]
    count = lax.axis_size("pair")
    place = lax.axis_index("pair").astype(jnp.int32).reshape(1, 1)
    block, packed = (rows, HALF), (PACKED_ROWS, LANES)
    line = list(range(count))
    odd_edges, even_edges = list(zip(line[1:-1:2], line[2::2])), list(zip(line[::2], line[1::2]))
    cycle = line[::2] + line[::-2]
    x_edges = list(zip(cycle[::2], cycle[1::2]))
    y_edges = list(zip(cycle[1::2], cycle[2::2] + cycle[:1]))

    top, bottom, band = call(
        start_kernel,
        [place, snapshots],
        [block, block, packed],
        [pltpu.VMEM((rows, 2 * HALF), jnp.float32), pltpu.SemaphoreType.DMA((4,))],
        pltpu.HBM,
    )
    kept, odd, even = call(
        rotate_kernel, [place, top, bottom, row_parts_of_ring(band)], [block] * 3
    )
    top, bottom, band = call(
        functools.partial(arrive_kernel, count),
        [place, kept, exchange(odd, odd_edges), exchange(even, even_edges)],
        [block, block, packed],
    )
    y, x = call(
        functools.partial(rotate_far_kernel, count),
        [place, top, bottom, row_parts_of_ring(band)],
        [block] * 2,
    )
    y_in = exchange(y, y_edges)
    x_in = exchange(x, x_edges)
    *blocks, band = call(
        functools.partial(arrive_far_kernel, count),
        [place, y, x, y_in, x_in],
        [block] * 4 + [(2 * PACKED_ROWS, LANES)],
    )
    (out,) = call(
        functools.partial(finish_kernel, count),
        [place, *blocks, row_parts(band)],
        [(rows, 2 * HALF)],
    )
    return out


def solution(mesh):
    pairs, rows = mesh.devices.shape
    fine = Mesh(mesh.devices.reshape(pairs, 2, rows // 4, 2), ("pair", "half", "far", "near"))
    spec = P(("half", "far", "near"), "pair")
    return jax.shard_map(
        per_device, mesh=fine, in_specs=(spec,), out_specs=spec, check_vma=False
    )
```

```python
import functools

import jax
import jax.numpy as jnp
from jax import lax
from jax.experimental import pallas as pl
from jax.experimental.pallas import tpu as pltpu
from jax.sharding import Mesh, PartitionSpec as P

HALF = 256
LANES = 128
BANDS = 11
PACKED_ROWS = 24
CHUNK = 8


def lanes_of(x):
    return lax.broadcasted_iota(jnp.int32, x.shape, 1)


def roll(x, by):
    return pltpu.roll(x, by % HALF, 1)


def halves(x):
    return x[:, :LANES], x[:, LANES:]


def reverse(x):
    left, right = halves(x)
    return jnp.concatenate([right, left], axis=1)


def split(top, bottom):
    (top_left, top_right), (bottom_left, bottom_right) = halves(top), halves(bottom)
    ahead = jnp.concatenate([top_left, bottom_right], axis=1)
    back = jnp.concatenate([bottom_left, top_right], axis=1)
    return ahead, back


def pick(x, index):
    return jnp.take_along_axis(x, index, axis=1)


def to_cycle(x):
    left, right = halves(x)
    lane = lanes_of(left)
    up, down = 2 * lane % LANES, (2 * LANES - 1 - 2 * lane) % LANES
    first = lane < LANES // 2
    return jnp.concatenate(
        [
            jnp.where(first, pick(left, up), pick(right, up)),
            jnp.where(first, pick(right, down), pick(left, down)),
        ],
        axis=1,
    )


def from_cycle(x):
    left, right = halves(x)
    lane = lanes_of(left)
    half = lane // 2
    even = lane % 2 == 0
    low = jnp.where(even, pick(left, half), pick(right, LANES - 1 - half))
    high = jnp.where(even, pick(left, LANES // 2 + half), pick(right, LANES // 2 - 1 - half))
    return jnp.concatenate([low, high], axis=1)


def turn(ahead, back, matrix):
    m00, m01, m10, m11 = matrix
    return m00 * ahead + m01 * back, m10 * ahead + m11 * back


def swap_at(lane, ahead, back):
    here = lanes_of(ahead) == lane
    return jnp.where(here, back, ahead), jnp.where(here, ahead, back)


def band_products(top, bottom):
    f, b = split(top, bottom)
    f1, b1, f2, b2 = roll(f, -1), roll(b, -1), roll(f, -2), roll(b, -2)
    return f * f, b * b, f * b, f * f1, f * b1, b * f1, b * b1, f * f2, f * b2, b * f2, b * b2


def bands_of(read, rows):
    total = None
    for start in range(0, rows, CHUNK):
        terms = band_products(*read(start))
        total = terms if total is None else [t + u for t, u in zip(total, terms)]
    return [jnp.sum(t, axis=0, keepdims=True) for t in total]


def pack(*pair_bands):
    left = [bands[k][:, :LANES] for k in range(BANDS) for bands in pair_bands]
    right = [bands[k][:, LANES:] for k in range(BANDS) for bands in pair_bands]
    blank = jnp.zeros((len(pair_bands) * (PACKED_ROWS - 2 * BANDS), LANES), jnp.float32)
    return jnp.concatenate(left + right + [blank], axis=0)


def unpack(packed):
    count = packed.shape[0] // PACKED_ROWS
    rows = [packed[k * count : (k + 1) * count] for k in range(2 * BANDS)]
    return [jnp.concatenate([rows[k], rows[BANDS + k]], axis=1) for k in range(BANDS)]


def matrix_of(ff, bb, fb, upper_ahead, swapped_lane):
    a, b, c = jnp.where(upper_ahead, ff, bb), jnp.where(upper_ahead, bb, ff), fb
    difference = b - a
    sign = jnp.where(difference >= 0, 1.0, -1.0)
    radius = jnp.sqrt(difference * difference + 4.0 * c * c + (1e-06 * (a + b)) ** 2)
    tangent = 2.0 * c * sign / (jnp.abs(difference) + radius)
    cosine = 1.0 / jnp.sqrt(1.0 + tangent * tangent)
    sine = tangent * cosine
    sine = jnp.where(upper_ahead, sine, -sine)
    if swapped_lane is None:
        return cosine, -sine, sine, cosine
    here = lanes_of(ff) == swapped_lane
    rows = jnp.where(here, sine, cosine), jnp.where(here, cosine, sine)
    return rows[0], jnp.where(here, cosine, -sine), rows[1], jnp.where(here, -sine, cosine)


def turn_diagonal(ff, bb, fb, matrix):
    m00, m01, m10, m11 = matrix
    return (
        m00 * m00 * ff + 2.0 * m00 * m01 * fb + m01 * m01 * bb,
        m10 * m10 * ff + 2.0 * m10 * m11 * fb + m11 * m11 * bb,
        m00 * m10 * ff + (m00 * m11 + m01 * m10) * fb + m01 * m11 * bb,
    )


def turn_block(block, left, right):
    ff, fb, bf, bb = block
    ff, bf = turn(ff, bf, left)
    fb, bb = turn(fb, bb, left)
    ff, fb = turn(ff, fb, right)
    bf, bb = turn(bf, bb, right)
    return ff, fb, bf, bb


def shifted(matrix, by):
    return [roll(m, -by) for m in matrix]


def three_matrices(packed):
    rows = unpack(packed)
    lane = lanes_of(rows[0])
    left = lane < LANES
    first = matrix_of(*rows[:3], left, 0)
    ff, bb, fb = turn_diagonal(*rows[:3], first)
    near_ff, near_fb, _, near_bb = turn_block(rows[3:7], first, shifted(first, 1))
    _, far_fb, _, _ = turn_block(rows[7:11], first, shifted(first, 2))
    diagonal = ff, roll(bb, -1), near_fb
    second = matrix_of(*diagonal, left, HALF - 1)
    block = near_ff, far_fb, roll(fb, -1), roll(near_bb, -1)
    ff, bb, _ = turn_diagonal(*diagonal, second)
    _, cross, _, _ = turn_block(block, second, shifted(second, 1))
    upper_ahead = (lane < LANES - 1) | (lane == HALF - 1)
    return first, second, matrix_of(ff, roll(bb, -1), cross, upper_ahead, None)


def ordered_sum(x):
    return functools.reduce(jnp.add, [x[i] for i in range(x.shape[0])])


def chosen(condition, x, y):
    return jnp.where(condition, x, y)


def wide(matrices, index=0):
    row = slice(index, index + 1)
    return [[jnp.broadcast_to(v[row], (CHUNK, HALF)) for v in matrix] for matrix in matrices]


def rotated(top, bottom, matrices):
    first, second, third = matrices
    ahead, back = turn(*split(top, bottom), first)
    ahead, back = turn(ahead, roll(back, -1), second)
    ahead, back = turn(ahead, roll(back, -1), third)
    ahead, back = swap_at(HALF - 1, ahead, roll(back, 1))
    return split(*swap_at(0, ahead, roll(back, 1)))


def chunks(ref):
    return [pl.ds(start, CHUNK) for start in range(0, ref.shape[0], CHUNK)]


def start_kernel(place_ref, work_ref, top_ref, bottom_ref, band_ref):
    def read(start):
        row = pl.ds(start, CHUNK)
        top = to_cycle(work_ref[row, :HALF])
        bottom = reverse(to_cycle(work_ref[row, HALF:]))
        top_ref[row, :] = top
        bottom_ref[row, :] = bottom
        return top, bottom

    band_ref[...] = pack(bands_of(read, work_ref.shape[0]))


def rotate_kernel(place_ref, top_ref, bottom_ref, parts_ref, kept_ref, odd_ref, even_ref):
    place = place_ref[0, 0]
    at_odd = place % 2 == 1
    matrices = wide(three_matrices(ordered_sum(parts_ref)))
    for row in chunks(top_ref):
        top, bottom = rotated(top_ref[row, :], bottom_ref[row, :], matrices)
        right = chosen(place == 0, reverse(bottom), top)
        kept_ref[row, :] = chosen(place == 0, top, reverse(top))
        odd_ref[row, :] = chosen(at_odd, right, bottom)
        even_ref[row, :] = chosen(at_odd, bottom, right)


def arrive_kernel(count, place_ref, kept_ref, odd_ref, even_ref, top_ref, bottom_ref, band_ref):
    place = place_ref[0, 0]
    at_odd = place % 2 == 1

    def read(start):
        row = pl.ds(start, CHUNK)
        kept, odd, even = kept_ref[row, :], odd_ref[row, :], even_ref[row, :]
        top = chosen(place == 0, kept, chosen(at_odd, even, odd))
        bottom = chosen(place == count - 1, kept, chosen(at_odd, odd, even))
        top_ref[row, :] = top
        bottom_ref[row, :] = bottom
        return top, bottom

    band_ref[...] = pack(bands_of(read, kept_ref.shape[0]))


def rotate_far_kernel(count, place_ref, top_ref, bottom_ref, parts_ref, x_ref, y_ref, late_ref):
    place = place_ref[0, 0]
    low = place % 4 < 2
    matrices = wide(three_matrices(ordered_sum(parts_ref)))
    for row in chunks(top_ref):
        top, bottom = rotated(top_ref[row, :], bottom_ref[row, :], matrices)
        flip = reverse(chosen(place == 0, bottom, top))
        upper = chosen((place == 0) | (place == count - 1), flip, top)
        lower = chosen(place == 0, top, bottom)
        x = chosen(low, upper, lower)
        x_ref[row, :] = x
        y_ref[row, :] = chosen(low, lower, upper)
        late_ref[row, :] = x


def late_edges(count):
    middle = count // 2
    return [(middle, middle + 2), (middle - 1, middle - 3)]


def arrive_far_kernel(count, place_ref, x_ref, y_ref, late_ref, x_in_ref, y_in_ref, late_in_ref, *refs):
    before_refs, after_refs, band_ref = refs[:2], refs[2:4], refs[4]
    place = place_ref[0, 0]
    low = place % 4 < 2
    start_end, last_end = place == 0, place == count - 1
    late = functools.reduce(jnp.logical_or, [place == i for i in sum(late_edges(count), ())])

    def read_before(start):
        row = pl.ds(start, CHUNK)
        x, y, y_in = x_ref[row, :], y_ref[row, :], y_in_ref[row, :]
        x_in = chosen(late, late_in_ref[row, :], x_in_ref[row, :])
        top = chosen(start_end, y, chosen(low, y_in, x_in))
        bottom = chosen(start_end, y_in, chosen(low, y, x))
        before_refs[0][row, :] = top
        before_refs[1][row, :] = bottom
        return top, bottom

    def read_after(start):
        row = pl.ds(start, CHUNK)
        x, y, y_in = x_ref[row, :], y_ref[row, :], y_in_ref[row, :]
        x_in = chosen(late, late_in_ref[row, :], x_in_ref[row, :])
        top = chosen(low, x, chosen(last_end, y_in, y))
        bottom = chosen(low, x_in, chosen(last_end, y, y_in))
        after_refs[0][row, :] = top
        after_refs[1][row, :] = bottom
        return top, bottom

    rows = x_ref.shape[0]
    band_ref[...] = pack(bands_of(read_before, rows), bands_of(read_after, rows))


def finish_kernel(
    count, place_ref, top_before_ref, bottom_before_ref, top_after_ref, bottom_after_ref, parts_ref, out_ref
):
    place = place_ref[0, 0]
    both = three_matrices(ordered_sum(parts_ref))
    matrices_before, matrices_after = wide(both, 0), wide(both, 1)
    for row in chunks(out_ref):
        top, bottom = rotated(top_before_ref[row, :], bottom_before_ref[row, :], matrices_before)
        out_ref[row, :HALF] = from_cycle(chosen(place == 1, reverse(bottom), top))
        top, bottom = rotated(top_after_ref[row, :], bottom_after_ref[row, :], matrices_after)
        out_ref[row, HALF:] = from_cycle(chosen(place == count - 1, top, reverse(bottom)))


def call(kernel, inputs, outputs):
    spec = pl.BlockSpec(memory_space=pltpu.VMEM)
    return pl.pallas_call(
        kernel,
        in_specs=[pl.BlockSpec(memory_space=pltpu.SMEM)] + [spec] * (len(inputs) - 1),
        out_specs=[spec] * len(outputs),
        out_shape=[jax.ShapeDtypeStruct(shape, jnp.float32) for shape in outputs],
        compiler_params=pltpu.CompilerParams(vmem_limit_bytes=8 * 1024 * 1024),
    )(*inputs)


def from_all(x, axes, first=0):
    count = lax.axis_size(axes)
    copies = jnp.broadcast_to(x[None], (count, *x.shape))
    order = [(first + i) % count for i in range(count)]
    groups = [order] if first else None
    return lax.all_to_all(copies, axes, 0, 0, tiled=True, axis_index_groups=groups)


def row_parts(x):
    near = ordered_sum(from_all(x, ("half", "near")))
    return from_all(near, "far", lax.axis_size("far") // 2)


def exchange(x, edges):
    return lax.ppermute(x, "pair", edges + [(j, i) for i, j in edges])


def per_device(snapshots):
    rows = snapshots.shape[0]
    count = lax.axis_size("pair")
    place = lax.axis_index("pair").astype(jnp.int32).reshape(1, 1)
    block, packed = (rows, HALF), (PACKED_ROWS, LANES)
    line = list(range(count))
    odd_edges, even_edges = list(zip(line[1:-1:2], line[2::2])), list(zip(line[::2], line[1::2]))
    cycle = line[::2] + line[::-2]
    x_edges = list(zip(cycle[::2], cycle[1::2]))
    y_edges = list(zip(cycle[1::2], cycle[2::2] + cycle[:1]))

    top, bottom, band = call(start_kernel, [place, snapshots], [block, block, packed])
    kept, odd, even = call(
        rotate_kernel, [place, top, bottom, row_parts(band)], [block] * 3
    )
    top, bottom, band = call(
        functools.partial(arrive_kernel, count),
        [place, kept, exchange(odd, odd_edges), exchange(even, even_edges)],
        [block, block, packed],
    )
    x, y, late = call(
        functools.partial(rotate_far_kernel, count),
        [place, top, bottom, row_parts(band)],
        [block] * 3,
    )
    x_in = exchange(x, [edge for edge in x_edges if edge not in late_edges(count)])
    y_in = exchange(y, y_edges)
    late_in = exchange(late, late_edges(count))
    *blocks, band = call(
        functools.partial(arrive_far_kernel, count),
        [place, x, y, late, x_in, y_in, late_in],
        [block] * 4 + [(2 * PACKED_ROWS, LANES)],
    )
    (out,) = call(
        functools.partial(finish_kernel, count),
        [place, *blocks, row_parts(band)],
        [(rows, 2 * HALF)],
    )
    return out


def solution(mesh):
    pairs, rows = mesh.devices.shape
    fine = Mesh(mesh.devices.reshape(pairs, 2, rows // 4, 2), ("pair", "half", "far", "near"))
    spec = P(("half", "far", "near"), "pair")
    return jax.shard_map(
        per_device, mesh=fine, in_specs=(spec,), out_specs=spec, check_vma=False
    )
```

```python
import functools

import jax
import jax.numpy as jnp
from jax import lax
from jax.experimental import pallas as pl
from jax.experimental.pallas import tpu as pltpu
from jax.sharding import Mesh, PartitionSpec as P

HALF = 256
LANES = 128
BANDS = 11
PACKED_ROWS = 24
CHUNK = 8


def lanes_of(x):
    return lax.broadcasted_iota(jnp.int32, x.shape, 1)


def roll(x, by):
    return pltpu.roll(x, by % HALF, 1)


def halves(x):
    return x[:, :LANES], x[:, LANES:]


def reverse(x):
    left, right = halves(x)
    return jnp.concatenate([right, left], axis=1)


def split(top, bottom):
    (top_left, top_right), (bottom_left, bottom_right) = halves(top), halves(bottom)
    ahead = jnp.concatenate([top_left, bottom_right], axis=1)
    back = jnp.concatenate([bottom_left, top_right], axis=1)
    return ahead, back


def pick(x, index):
    return jnp.take_along_axis(x, index, axis=1)


def to_cycle(x):
    left, right = halves(x)
    lane = lanes_of(left)
    first = lane < LANES // 2
    evens_then_odds = jnp.where(first, 2 * lane, 2 * LANES - 1 - 2 * lane)
    left = pick(left, evens_then_odds)
    right = pltpu.roll(pick(right, evens_then_odds), LANES // 2, 1)
    return jnp.concatenate([jnp.where(first, left, right), jnp.where(first, right, left)], axis=1)


def from_cycle(x):
    up, down = halves(x)
    lane = lanes_of(up)
    first = lane < LANES // 2
    left = jnp.where(first, up, down)
    right = pltpu.roll(jnp.where(first, down, up), LANES // 2, 1)
    place = jnp.where(lane % 2 == 0, lane // 2, LANES - 1 - lane // 2)
    return jnp.concatenate([pick(left, place), pick(right, place)], axis=1)


def turn(ahead, back, matrix):
    m00, m01, m10, m11 = matrix
    return m00 * ahead + m01 * back, m10 * ahead + m11 * back


def swap_at(lane, ahead, back):
    here = lanes_of(ahead) == lane
    return jnp.where(here, back, ahead), jnp.where(here, ahead, back)


def band_products(top, bottom):
    f, b = split(top, bottom)
    f1, b1, f2, b2 = roll(f, -1), roll(b, -1), roll(f, -2), roll(b, -2)
    return f * f, b * b, f * b, f * f1, f * b1, b * f1, b * b1, f * f2, f * b2, b * f2, b * b2


def bands_of(read, rows):
    total = None
    for start in range(0, rows, CHUNK):
        terms = band_products(*read(start))
        total = terms if total is None else [t + u for t, u in zip(total, terms)]
    return [jnp.sum(t, axis=0, keepdims=True) for t in total]


def pack(*pair_bands):
    left = [bands[k][:, :LANES] for k in range(BANDS) for bands in pair_bands]
    right = [bands[k][:, LANES:] for k in range(BANDS) for bands in pair_bands]
    blank = jnp.zeros((len(pair_bands) * (PACKED_ROWS - 2 * BANDS), LANES), jnp.float32)
    return jnp.concatenate(left + right + [blank], axis=0)


def unpack(packed):
    count = packed.shape[0] // PACKED_ROWS
    rows = [packed[k * count : (k + 1) * count] for k in range(2 * BANDS)]
    return [jnp.concatenate([rows[k], rows[BANDS + k]], axis=1) for k in range(BANDS)]


def matrix_of(ff, bb, fb, upper_ahead, swapped_lane):
    a, b, c = jnp.where(upper_ahead, ff, bb), jnp.where(upper_ahead, bb, ff), fb
    difference = b - a
    sign = jnp.where(difference >= 0, 1.0, -1.0)
    radius = jnp.sqrt(difference * difference + 4.0 * c * c + (1e-06 * (a + b)) ** 2)
    tangent = 2.0 * c * sign / (jnp.abs(difference) + radius)
    cosine = 1.0 / jnp.sqrt(1.0 + tangent * tangent)
    sine = tangent * cosine
    sine = jnp.where(upper_ahead, sine, -sine)
    if swapped_lane is None:
        return cosine, -sine, sine, cosine
    here = lanes_of(ff) == swapped_lane
    rows = jnp.where(here, sine, cosine), jnp.where(here, cosine, sine)
    return rows[0], jnp.where(here, cosine, -sine), rows[1], jnp.where(here, -sine, cosine)


def turn_diagonal(ff, bb, fb, matrix):
    m00, m01, m10, m11 = matrix
    return (
        m00 * m00 * ff + 2.0 * m00 * m01 * fb + m01 * m01 * bb,
        m10 * m10 * ff + 2.0 * m10 * m11 * fb + m11 * m11 * bb,
        m00 * m10 * ff + (m00 * m11 + m01 * m10) * fb + m01 * m11 * bb,
    )


def turn_block(block, left, right):
    ff, fb, bf, bb = block
    ff, bf = turn(ff, bf, left)
    fb, bb = turn(fb, bb, left)
    ff, fb = turn(ff, fb, right)
    bf, bb = turn(bf, bb, right)
    return ff, fb, bf, bb


def shifted(matrix, by):
    return [roll(m, -by) for m in matrix]


def three_matrices(packed):
    rows = unpack(packed)
    lane = lanes_of(rows[0])
    left = lane < LANES
    first = matrix_of(*rows[:3], left, 0)
    ff, bb, fb = turn_diagonal(*rows[:3], first)
    near_ff, near_fb, _, near_bb = turn_block(rows[3:7], first, shifted(first, 1))
    _, far_fb, _, _ = turn_block(rows[7:11], first, shifted(first, 2))
    diagonal = ff, roll(bb, -1), near_fb
    second = matrix_of(*diagonal, left, HALF - 1)
    block = near_ff, far_fb, roll(fb, -1), roll(near_bb, -1)
    ff, bb, _ = turn_diagonal(*diagonal, second)
    _, cross, _, _ = turn_block(block, second, shifted(second, 1))
    upper_ahead = (lane < LANES - 1) | (lane == HALF - 1)
    return first, second, matrix_of(ff, roll(bb, -1), cross, upper_ahead, None)


def ordered_sum(x):
    return functools.reduce(jnp.add, [x[i] for i in range(x.shape[0])])


def chosen(condition, x, y):
    return jnp.where(condition, x, y)


def wide(matrices, index=0):
    row = slice(index, index + 1)
    return [[jnp.broadcast_to(v[row], (CHUNK, HALF)) for v in matrix] for matrix in matrices]


def rotated(top, bottom, matrices):
    first, second, third = matrices
    ahead, back = turn(*split(top, bottom), first)
    ahead, back = turn(ahead, roll(back, -1), second)
    ahead, back = turn(ahead, roll(back, -1), third)
    ahead, back = swap_at(HALF - 1, ahead, roll(back, 1))
    return split(*swap_at(0, ahead, roll(back, 1)))


def chunks(ref):
    return [pl.ds(start, CHUNK) for start in range(0, ref.shape[0], CHUNK)]


def start_kernel(place_ref, work_ref, top_ref, bottom_ref, band_ref):
    def read(start):
        row = pl.ds(start, CHUNK)
        top = to_cycle(work_ref[row, :HALF])
        bottom = reverse(to_cycle(work_ref[row, HALF:]))
        top_ref[row, :] = top
        bottom_ref[row, :] = bottom
        return top, bottom

    band_ref[...] = pack(bands_of(read, work_ref.shape[0]))


def rotate_kernel(place_ref, top_ref, bottom_ref, parts_ref, kept_ref, odd_ref, even_ref):
    place = place_ref[0, 0]
    at_odd = place % 2 == 1
    matrices = wide(three_matrices(ordered_sum(parts_ref)))
    for row in chunks(top_ref):
        top, bottom = rotated(top_ref[row, :], bottom_ref[row, :], matrices)
        right = chosen(place == 0, reverse(bottom), top)
        kept_ref[row, :] = chosen(place == 0, top, reverse(top))
        odd_ref[row, :] = chosen(at_odd, right, bottom)
        even_ref[row, :] = chosen(at_odd, bottom, right)


def arrive_kernel(count, place_ref, kept_ref, odd_ref, even_ref, top_ref, bottom_ref, band_ref):
    place = place_ref[0, 0]
    at_odd = place % 2 == 1

    def read(start):
        row = pl.ds(start, CHUNK)
        kept, odd, even = kept_ref[row, :], odd_ref[row, :], even_ref[row, :]
        top = chosen(place == 0, kept, chosen(at_odd, even, odd))
        bottom = chosen(place == count - 1, kept, chosen(at_odd, odd, even))
        top_ref[row, :] = top
        bottom_ref[row, :] = bottom
        return top, bottom

    band_ref[...] = pack(bands_of(read, kept_ref.shape[0]))


def rotate_far_kernel(count, place_ref, top_ref, bottom_ref, parts_ref, x_ref, y_ref, late_ref):
    place = place_ref[0, 0]
    low = place % 4 < 2
    matrices = wide(three_matrices(ordered_sum(parts_ref)))
    for row in chunks(top_ref):
        top, bottom = rotated(top_ref[row, :], bottom_ref[row, :], matrices)
        flip = reverse(chosen(place == 0, bottom, top))
        upper = chosen((place == 0) | (place == count - 1), flip, top)
        lower = chosen(place == 0, top, bottom)
        x = chosen(low, upper, lower)
        x_ref[row, :] = x
        y_ref[row, :] = chosen(low, lower, upper)
        late_ref[row, :] = x


def late_edges(count):
    middle = count // 2
    return [(middle, middle + 2), (middle - 1, middle - 3)]


def arrive_far_kernel(count, place_ref, x_ref, y_ref, late_ref, x_in_ref, y_in_ref, late_in_ref, *refs):
    before_refs, after_refs, band_ref = refs[:2], refs[2:4], refs[4]
    place = place_ref[0, 0]
    low = place % 4 < 2
    start_end, last_end = place == 0, place == count - 1
    late = functools.reduce(jnp.logical_or, [place == i for i in sum(late_edges(count), ())])

    def read_before(start):
        row = pl.ds(start, CHUNK)
        x, y, y_in = x_ref[row, :], y_ref[row, :], y_in_ref[row, :]
        x_in = chosen(late, late_in_ref[row, :], x_in_ref[row, :])
        top = chosen(start_end, y, chosen(low, y_in, x_in))
        bottom = chosen(start_end, y_in, chosen(low, y, x))
        before_refs[0][row, :] = top
        before_refs[1][row, :] = bottom
        return top, bottom

    def read_after(start):
        row = pl.ds(start, CHUNK)
        x, y, y_in = x_ref[row, :], y_ref[row, :], y_in_ref[row, :]
        x_in = chosen(late, late_in_ref[row, :], x_in_ref[row, :])
        top = chosen(low, x, chosen(last_end, y_in, y))
        bottom = chosen(low, x_in, chosen(last_end, y, y_in))
        after_refs[0][row, :] = top
        after_refs[1][row, :] = bottom
        return top, bottom

    rows = x_ref.shape[0]
    band_ref[...] = pack(bands_of(read_before, rows), bands_of(read_after, rows))


def finish_kernel(
    count, place_ref, top_before_ref, bottom_before_ref, top_after_ref, bottom_after_ref, parts_ref,
    out_hbm, out_ref, sems
):
    place = place_ref[0, 0]
    both = three_matrices(ordered_sum(parts_ref))
    matrices_before, matrices_after = wide(both, 0), wide(both, 1)
    size = out_ref.shape[0] // sems.shape[0]
    copies = []
    for i in range(sems.shape[0]):
        for start in range(i * size, (i + 1) * size, CHUNK):
            row = pl.ds(start, CHUNK)
            top, bottom = rotated(top_before_ref[row, :], bottom_before_ref[row, :], matrices_before)
            out_ref[row, :HALF] = from_cycle(chosen(place == 1, reverse(bottom), top))
            top, bottom = rotated(top_after_ref[row, :], bottom_after_ref[row, :], matrices_after)
            out_ref[row, HALF:] = from_cycle(chosen(place == count - 1, top, reverse(bottom)))
        part = pl.ds(i * size, size)
        copies.append(pltpu.make_async_copy(out_ref.at[part], out_hbm.at[part], sems.at[i]))
        copies[-1].start()
    for copy in copies:
        copy.wait()


def call(kernel, inputs, outputs, scratch=(), space=pltpu.VMEM):
    spec = pl.BlockSpec(memory_space=pltpu.VMEM)
    return pl.pallas_call(
        kernel,
        in_specs=[pl.BlockSpec(memory_space=pltpu.SMEM)] + [spec] * (len(inputs) - 1),
        out_specs=[pl.BlockSpec(memory_space=space)] * len(outputs),
        out_shape=[jax.ShapeDtypeStruct(shape, jnp.float32) for shape in outputs],
        scratch_shapes=list(scratch),
        compiler_params=pltpu.CompilerParams(vmem_limit_bytes=8 * 1024 * 1024),
    )(*inputs)


def from_all(x, axes, first=0):
    count = lax.axis_size(axes)
    copies = jnp.broadcast_to(x[None], (count, *x.shape))
    order = [(first + i) % count for i in range(count)]
    groups = [order] if first else None
    return lax.all_to_all(copies, axes, 0, 0, tiled=True, axis_index_groups=groups)


def row_parts(x):
    near = ordered_sum(from_all(x, ("half", "near")))
    return from_all(near, "far", lax.axis_size("far") // 2)


def exchange(x, edges):
    return lax.ppermute(x, "pair", edges + [(j, i) for i, j in edges])


def per_device(snapshots):
    rows = snapshots.shape[0]
    count = lax.axis_size("pair")
    place = lax.axis_index("pair").astype(jnp.int32).reshape(1, 1)
    block, packed = (rows, HALF), (PACKED_ROWS, LANES)
    line = list(range(count))
    odd_edges, even_edges = list(zip(line[1:-1:2], line[2::2])), list(zip(line[::2], line[1::2]))
    cycle = line[::2] + line[::-2]
    x_edges = list(zip(cycle[::2], cycle[1::2]))
    y_edges = list(zip(cycle[1::2], cycle[2::2] + cycle[:1]))

    top, bottom, band = call(start_kernel, [place, snapshots], [block, block, packed])
    kept, odd, even = call(
        rotate_kernel, [place, top, bottom, row_parts(band)], [block] * 3
    )
    top, bottom, band = call(
        functools.partial(arrive_kernel, count),
        [place, kept, exchange(odd, odd_edges), exchange(even, even_edges)],
        [block, block, packed],
    )
    x, y, late = call(
        functools.partial(rotate_far_kernel, count),
        [place, top, bottom, row_parts(band)],
        [block] * 3,
    )
    x_in = exchange(x, [edge for edge in x_edges if edge not in late_edges(count)])
    y_in = exchange(y, y_edges)
    late_in = exchange(late, late_edges(count))
    *blocks, band = call(
        functools.partial(arrive_far_kernel, count),
        [place, x, y, late, x_in, y_in, late_in],
        [block] * 4 + [(2 * PACKED_ROWS, LANES)],
    )
    (out,) = call(
        functools.partial(finish_kernel, count),
        [place, *blocks, row_parts(band)],
        [(rows, 2 * HALF)],
        [pltpu.VMEM((rows, 2 * HALF), jnp.float32), pltpu.SemaphoreType.DMA((4,))],
        pltpu.HBM,
    )
    return out


def solution(mesh):
    pairs, rows = mesh.devices.shape
    fine = Mesh(mesh.devices.reshape(pairs, 2, rows // 4, 2), ("pair", "half", "far", "near"))
    spec = P(("half", "far", "near"), "pair")
    return jax.shard_map(
        per_device, mesh=fine, in_specs=(spec,), out_specs=spec, check_vma=False
    )
```

```python
import functools

import jax
import jax.numpy as jnp
from jax import lax
from jax.experimental import pallas as pl
from jax.experimental.pallas import tpu as pltpu
from jax.sharding import Mesh, PartitionSpec as P

HALF = 256
LANES = 128
BANDS = 11
PACKED_ROWS = 24
CHUNK = 8


def lanes_of(x):
    return lax.broadcasted_iota(jnp.int32, x.shape, 1)


def roll(x, by):
    return pltpu.roll(x, by % HALF, 1)


def halves(x):
    return x[:, :LANES], x[:, LANES:]


def reverse(x):
    left, right = halves(x)
    return jnp.concatenate([right, left], axis=1)


def split(top, bottom):
    (top_left, top_right), (bottom_left, bottom_right) = halves(top), halves(bottom)
    ahead = jnp.concatenate([top_left, bottom_right], axis=1)
    back = jnp.concatenate([bottom_left, top_right], axis=1)
    return ahead, back


def pick(x, index):
    return jnp.take_along_axis(x, index, axis=1)


def to_cycle(x):
    left, right = halves(x)
    lane = lanes_of(left)
    first = lane < LANES // 2
    evens_then_odds = jnp.where(first, 2 * lane, 2 * LANES - 1 - 2 * lane)
    left = pick(left, evens_then_odds)
    right = pltpu.roll(pick(right, evens_then_odds), LANES // 2, 1)
    return jnp.concatenate([jnp.where(first, left, right), jnp.where(first, right, left)], axis=1)


def from_cycle(x):
    up, down = halves(x)
    lane = lanes_of(up)
    first = lane < LANES // 2
    left = jnp.where(first, up, down)
    right = pltpu.roll(jnp.where(first, down, up), LANES // 2, 1)
    place = jnp.where(lane % 2 == 0, lane // 2, LANES - 1 - lane // 2)
    return jnp.concatenate([pick(left, place), pick(right, place)], axis=1)


def turn(ahead, back, matrix):
    m00, m01, m10, m11 = matrix
    return m00 * ahead + m01 * back, m10 * ahead + m11 * back


def swap_at(lane, ahead, back):
    here = lanes_of(ahead) == lane
    return jnp.where(here, back, ahead), jnp.where(here, ahead, back)


def band_products(top, bottom):
    f, b = split(top, bottom)
    f1, b1, f2, b2 = roll(f, -1), roll(b, -1), roll(f, -2), roll(b, -2)
    return f * f, b * b, f * b, f * f1, f * b1, b * f1, b * b1, f * f2, f * b2, b * f2, b * b2


def bands_of(read, rows):
    total = None
    for start in range(0, rows, CHUNK):
        terms = band_products(*read(start))
        total = terms if total is None else [t + u for t, u in zip(total, terms)]
    return [jnp.sum(t, axis=0, keepdims=True) for t in total]


def pack(*pair_bands):
    left = [bands[k][:, :LANES] for k in range(BANDS) for bands in pair_bands]
    right = [bands[k][:, LANES:] for k in range(BANDS) for bands in pair_bands]
    blank = jnp.zeros((len(pair_bands) * (PACKED_ROWS - 2 * BANDS), LANES), jnp.float32)
    return jnp.concatenate(left + right + [blank], axis=0)


def unpack(packed):
    count = packed.shape[0] // PACKED_ROWS
    rows = [packed[k * count : (k + 1) * count] for k in range(2 * BANDS)]
    return [jnp.concatenate([rows[k], rows[BANDS + k]], axis=1) for k in range(BANDS)]


def matrix_of(ff, bb, fb, upper_ahead, swapped_lane):
    a, b, c = jnp.where(upper_ahead, ff, bb), jnp.where(upper_ahead, bb, ff), fb
    difference = b - a
    sign = jnp.where(difference >= 0, 1.0, -1.0)
    radius = jnp.sqrt(difference * difference + 4.0 * c * c + (1e-06 * (a + b)) ** 2)
    tangent = 2.0 * c * sign / (jnp.abs(difference) + radius)
    cosine = 1.0 / jnp.sqrt(1.0 + tangent * tangent)
    sine = tangent * cosine
    sine = jnp.where(upper_ahead, sine, -sine)
    if swapped_lane is None:
        return cosine, -sine, sine, cosine
    here = lanes_of(ff) == swapped_lane
    rows = jnp.where(here, sine, cosine), jnp.where(here, cosine, sine)
    return rows[0], jnp.where(here, cosine, -sine), rows[1], jnp.where(here, -sine, cosine)


def turn_diagonal(ff, bb, fb, matrix):
    m00, m01, m10, m11 = matrix
    return (
        m00 * m00 * ff + 2.0 * m00 * m01 * fb + m01 * m01 * bb,
        m10 * m10 * ff + 2.0 * m10 * m11 * fb + m11 * m11 * bb,
        m00 * m10 * ff + (m00 * m11 + m01 * m10) * fb + m01 * m11 * bb,
    )


def turn_block(block, left, right):
    ff, fb, bf, bb = block
    ff, bf = turn(ff, bf, left)
    fb, bb = turn(fb, bb, left)
    ff, fb = turn(ff, fb, right)
    bf, bb = turn(bf, bb, right)
    return ff, fb, bf, bb


def shifted(matrix, by):
    return [roll(m, -by) for m in matrix]


def three_matrices(packed):
    rows = unpack(packed)
    lane = lanes_of(rows[0])
    left = lane < LANES
    first = matrix_of(*rows[:3], left, 0)
    ff, bb, fb = turn_diagonal(*rows[:3], first)
    near_ff, near_fb, _, near_bb = turn_block(rows[3:7], first, shifted(first, 1))
    _, far_fb, _, _ = turn_block(rows[7:11], first, shifted(first, 2))
    diagonal = ff, roll(bb, -1), near_fb
    second = matrix_of(*diagonal, left, HALF - 1)
    block = near_ff, far_fb, roll(fb, -1), roll(near_bb, -1)
    ff, bb, _ = turn_diagonal(*diagonal, second)
    _, cross, _, _ = turn_block(block, second, shifted(second, 1))
    upper_ahead = (lane < LANES - 1) | (lane == HALF - 1)
    return first, second, matrix_of(ff, roll(bb, -1), cross, upper_ahead, None)


def ordered_sum(x):
    return functools.reduce(jnp.add, [x[i] for i in range(x.shape[0])])


def chosen(condition, x, y):
    return jnp.where(condition, x, y)


def wide(matrices, index=0):
    row = slice(index, index + 1)
    return [[jnp.broadcast_to(v[row], (CHUNK, HALF)) for v in matrix] for matrix in matrices]


def rotated(top, bottom, matrices):
    first, second, third = matrices
    ahead, back = turn(*split(top, bottom), first)
    ahead, back = turn(ahead, roll(back, -1), second)
    ahead, back = turn(ahead, roll(back, -1), third)
    ahead, back = swap_at(HALF - 1, ahead, roll(back, 1))
    return split(*swap_at(0, ahead, roll(back, 1)))


def chunks(ref):
    return [pl.ds(start, CHUNK) for start in range(0, ref.shape[0], CHUNK)]


def start_kernel(place_ref, work_hbm, top_ref, bottom_ref, band_ref, work_ref, sems):
    rows = work_ref.shape[0]
    size = rows // sems.shape[0]
    copies = []
    for i in range(sems.shape[0]):
        part = pl.ds(i * size, size)
        copies.append(pltpu.make_async_copy(work_hbm.at[part], work_ref.at[part], sems.at[i]))
        copies[-1].start()

    def read(start):
        if start % size == 0:
            copies[start // size].wait()
        row = pl.ds(start, CHUNK)
        top = to_cycle(work_ref[row, :HALF])
        bottom = reverse(to_cycle(work_ref[row, HALF:]))
        top_ref[row, :] = top
        bottom_ref[row, :] = bottom
        return top, bottom

    band_ref[...] = pack(bands_of(read, rows))


def rotate_kernel(place_ref, top_ref, bottom_ref, parts_ref, kept_ref, odd_ref, even_ref):
    place = place_ref[0, 0]
    at_odd = place % 2 == 1
    matrices = wide(three_matrices(ordered_sum(parts_ref)))
    for row in chunks(top_ref):
        top, bottom = rotated(top_ref[row, :], bottom_ref[row, :], matrices)
        right = chosen(place == 0, reverse(bottom), top)
        kept_ref[row, :] = chosen(place == 0, top, reverse(top))
        odd_ref[row, :] = chosen(at_odd, right, bottom)
        even_ref[row, :] = chosen(at_odd, bottom, right)


def arrive_kernel(count, place_ref, kept_ref, odd_ref, even_ref, top_ref, bottom_ref, band_ref):
    place = place_ref[0, 0]
    at_odd = place % 2 == 1

    def read(start):
        row = pl.ds(start, CHUNK)
        kept, odd, even = kept_ref[row, :], odd_ref[row, :], even_ref[row, :]
        top = chosen(place == 0, kept, chosen(at_odd, even, odd))
        bottom = chosen(place == count - 1, kept, chosen(at_odd, odd, even))
        top_ref[row, :] = top
        bottom_ref[row, :] = bottom
        return top, bottom

    band_ref[...] = pack(bands_of(read, kept_ref.shape[0]))


def rotate_far_kernel(count, place_ref, top_ref, bottom_ref, parts_ref, x_ref, y_ref, late_ref):
    place = place_ref[0, 0]
    low = place % 4 < 2
    matrices = wide(three_matrices(ordered_sum(parts_ref)))
    for row in chunks(top_ref):
        top, bottom = rotated(top_ref[row, :], bottom_ref[row, :], matrices)
        flip = reverse(chosen(place == 0, bottom, top))
        upper = chosen((place == 0) | (place == count - 1), flip, top)
        lower = chosen(place == 0, top, bottom)
        x = chosen(low, upper, lower)
        x_ref[row, :] = x
        y_ref[row, :] = chosen(low, lower, upper)
        late_ref[row, :] = x


def late_edges(count):
    middle = count // 2
    return [(middle, middle + 2), (middle - 1, middle - 3)]


def arrive_far_kernel(count, place_ref, x_ref, y_ref, late_ref, x_in_ref, y_in_ref, late_in_ref, *refs):
    before_refs, after_refs, band_ref = refs[:2], refs[2:4], refs[4]
    place = place_ref[0, 0]
    low = place % 4 < 2
    start_end, last_end = place == 0, place == count - 1
    late = functools.reduce(jnp.logical_or, [place == i for i in sum(late_edges(count), ())])

    def read_before(start):
        row = pl.ds(start, CHUNK)
        x, y, y_in = x_ref[row, :], y_ref[row, :], y_in_ref[row, :]
        x_in = chosen(late, late_in_ref[row, :], x_in_ref[row, :])
        top = chosen(start_end, y, chosen(low, y_in, x_in))
        bottom = chosen(start_end, y_in, chosen(low, y, x))
        before_refs[0][row, :] = top
        before_refs[1][row, :] = bottom
        return top, bottom

    def read_after(start):
        row = pl.ds(start, CHUNK)
        x, y, y_in = x_ref[row, :], y_ref[row, :], y_in_ref[row, :]
        x_in = chosen(late, late_in_ref[row, :], x_in_ref[row, :])
        top = chosen(low, x, chosen(last_end, y_in, y))
        bottom = chosen(low, x_in, chosen(last_end, y, y_in))
        after_refs[0][row, :] = top
        after_refs[1][row, :] = bottom
        return top, bottom

    rows = x_ref.shape[0]
    band_ref[...] = pack(bands_of(read_before, rows), bands_of(read_after, rows))


def finish_kernel(
    count, place_ref, top_before_ref, bottom_before_ref, top_after_ref, bottom_after_ref, parts_ref,
    out_hbm, out_ref, sems
):
    place = place_ref[0, 0]
    both = three_matrices(ordered_sum(parts_ref))
    matrices_before, matrices_after = wide(both, 0), wide(both, 1)
    size = out_ref.shape[0] // sems.shape[0]
    copies = []
    for i in range(sems.shape[0]):
        for start in range(i * size, (i + 1) * size, CHUNK):
            row = pl.ds(start, CHUNK)
            top, bottom = rotated(top_before_ref[row, :], bottom_before_ref[row, :], matrices_before)
            out_ref[row, :HALF] = from_cycle(chosen(place == 1, reverse(bottom), top))
            top, bottom = rotated(top_after_ref[row, :], bottom_after_ref[row, :], matrices_after)
            out_ref[row, HALF:] = from_cycle(chosen(place == count - 1, top, reverse(bottom)))
        part = pl.ds(i * size, size)
        copies.append(pltpu.make_async_copy(out_ref.at[part], out_hbm.at[part], sems.at[i]))
        copies[-1].start()
    for copy in copies:
        copy.wait()


def call(kernel, inputs, outputs, scratch=(), source=pltpu.VMEM, target=pltpu.VMEM, limit=8):
    return pl.pallas_call(
        kernel,
        in_specs=[pl.BlockSpec(memory_space=pltpu.SMEM)] + [pl.BlockSpec(memory_space=source)] * (len(inputs) - 1),
        out_specs=[pl.BlockSpec(memory_space=target)] * len(outputs),
        out_shape=[jax.ShapeDtypeStruct(shape, jnp.float32) for shape in outputs],
        scratch_shapes=list(scratch),
        compiler_params=pltpu.CompilerParams(vmem_limit_bytes=limit * 1024 * 1024),
    )(*inputs)


def from_all(x, axes, first=0):
    count = lax.axis_size(axes)
    copies = jnp.broadcast_to(x[None], (count, *x.shape))
    order = [(first + i) % count for i in range(count)]
    groups = [order] if first else None
    return lax.all_to_all(copies, axes, 0, 0, tiled=True, axis_index_groups=groups)


def row_parts(x):
    near = ordered_sum(from_all(x, ("half", "near")))
    return from_all(near, "far", lax.axis_size("far") // 2)


def exchange(x, edges):
    return lax.ppermute(x, "pair", edges + [(j, i) for i, j in edges])


def per_device(snapshots):
    rows = snapshots.shape[0]
    count = lax.axis_size("pair")
    place = lax.axis_index("pair").astype(jnp.int32).reshape(1, 1)
    block, packed = (rows, HALF), (PACKED_ROWS, LANES)
    line = list(range(count))
    odd_edges, even_edges = list(zip(line[1:-1:2], line[2::2])), list(zip(line[::2], line[1::2]))
    cycle = line[::2] + line[::-2]
    x_edges = list(zip(cycle[::2], cycle[1::2]))
    y_edges = list(zip(cycle[1::2], cycle[2::2] + cycle[:1]))

    top, bottom, band = call(
        start_kernel,
        [place, snapshots],
        [block, block, packed],
        [pltpu.VMEM((rows, 2 * HALF), jnp.float32), pltpu.SemaphoreType.DMA((4,))],
        source=pltpu.HBM,
        limit=60,
    )
    kept, odd, even = call(
        rotate_kernel, [place, top, bottom, row_parts(band)], [block] * 3
    )
    top, bottom, band = call(
        functools.partial(arrive_kernel, count),
        [place, kept, exchange(odd, odd_edges), exchange(even, even_edges)],
        [block, block, packed],
    )
    x, y, late = call(
        functools.partial(rotate_far_kernel, count),
        [place, top, bottom, row_parts(band)],
        [block] * 3,
    )
    x_in = exchange(x, [edge for edge in x_edges if edge not in late_edges(count)])
    y_in = exchange(y, y_edges)
    late_in = exchange(late, late_edges(count))
    *blocks, band = call(
        functools.partial(arrive_far_kernel, count),
        [place, x, y, late, x_in, y_in, late_in],
        [block] * 4 + [(2 * PACKED_ROWS, LANES)],
    )
    (out,) = call(
        functools.partial(finish_kernel, count),
        [place, *blocks, row_parts(band)],
        [(rows, 2 * HALF)],
        [pltpu.VMEM((rows, 2 * HALF), jnp.float32), pltpu.SemaphoreType.DMA((4,))],
        target=pltpu.HBM,
    )
    return out


def solution(mesh):
    pairs, rows = mesh.devices.shape
    fine = Mesh(mesh.devices.reshape(pairs, 2, rows // 4, 2), ("pair", "half", "far", "near"))
    spec = P(("half", "far", "near"), "pair")
    return jax.shard_map(
        per_device, mesh=fine, in_specs=(spec,), out_specs=spec, check_vma=False
    )
```

```python
import functools

import jax
import jax.numpy as jnp
from jax import lax
from jax.experimental import pallas as pl
from jax.experimental.pallas import tpu as pltpu
from jax.sharding import Mesh, PartitionSpec as P

HALF = 256
LANES = 128
BANDS = 11
PACKED_ROWS = 24
CHUNK = 8


def lanes_of(x):
    return lax.broadcasted_iota(jnp.int32, x.shape, 1)


def roll(x, by):
    return pltpu.roll(x, by % HALF, 1)


def halves(x):
    return x[:, :LANES], x[:, LANES:]


def reverse(x):
    left, right = halves(x)
    return jnp.concatenate([right, left], axis=1)


def split(top, bottom):
    (top_left, top_right), (bottom_left, bottom_right) = halves(top), halves(bottom)
    ahead = jnp.concatenate([top_left, bottom_right], axis=1)
    back = jnp.concatenate([bottom_left, top_right], axis=1)
    return ahead, back


def pick(x, index):
    return jnp.take_along_axis(x, index, axis=1)


def to_cycle(x):
    left, right = halves(x)
    lane = lanes_of(left)
    first = lane < LANES // 2
    evens_then_odds = jnp.where(first, 2 * lane, 2 * LANES - 1 - 2 * lane)
    left = pick(left, evens_then_odds)
    right = pltpu.roll(pick(right, evens_then_odds), LANES // 2, 1)
    return jnp.concatenate([jnp.where(first, left, right), jnp.where(first, right, left)], axis=1)


def from_cycle(x):
    up, down = halves(x)
    lane = lanes_of(up)
    first = lane < LANES // 2
    left = jnp.where(first, up, down)
    right = pltpu.roll(jnp.where(first, down, up), LANES // 2, 1)
    place = jnp.where(lane % 2 == 0, lane // 2, LANES - 1 - lane // 2)
    return jnp.concatenate([pick(left, place), pick(right, place)], axis=1)


def turn(ahead, back, matrix):
    m00, m01, m10, m11 = matrix
    return m00 * ahead + m01 * back, m10 * ahead + m11 * back


def swap_at(lane, ahead, back):
    here = lanes_of(ahead) == lane
    return jnp.where(here, back, ahead), jnp.where(here, ahead, back)


def band_products(top, bottom):
    f, b = split(top, bottom)
    f1, b1, f2, b2 = roll(f, -1), roll(b, -1), roll(f, -2), roll(b, -2)
    return f * f, b * b, f * b, f * f1, f * b1, b * f1, b * b1, f * f2, f * b2, b * f2, b * b2


def bands_of(read, rows):
    total = None
    for start in range(0, rows, CHUNK):
        terms = band_products(*read(start))
        total = terms if total is None else [t + u for t, u in zip(total, terms)]
    return [jnp.sum(t, axis=0, keepdims=True) for t in total]


def pack(*pair_bands):
    left = [bands[k][:, :LANES] for k in range(BANDS) for bands in pair_bands]
    right = [bands[k][:, LANES:] for k in range(BANDS) for bands in pair_bands]
    blank = jnp.zeros((len(pair_bands) * (PACKED_ROWS - 2 * BANDS), LANES), jnp.float32)
    return jnp.concatenate(left + right + [blank], axis=0)


def unpack(packed):
    count = packed.shape[0] // PACKED_ROWS
    rows = [packed[k * count : (k + 1) * count] for k in range(2 * BANDS)]
    return [jnp.concatenate([rows[k], rows[BANDS + k]], axis=1) for k in range(BANDS)]


def matrix_of(ff, bb, fb, upper_ahead, swapped_lane):
    a, b, c = jnp.where(upper_ahead, ff, bb), jnp.where(upper_ahead, bb, ff), fb
    difference = b - a
    sign = jnp.where(difference >= 0, 1.0, -1.0)
    radius = jnp.sqrt(difference * difference + 4.0 * c * c + (1e-06 * (a + b)) ** 2)
    tangent = 2.0 * c * sign / (jnp.abs(difference) + radius)
    cosine = 1.0 / jnp.sqrt(1.0 + tangent * tangent)
    sine = tangent * cosine
    sine = jnp.where(upper_ahead, sine, -sine)
    if swapped_lane is None:
        return cosine, -sine, sine, cosine
    here = lanes_of(ff) == swapped_lane
    rows = jnp.where(here, sine, cosine), jnp.where(here, cosine, sine)
    return rows[0], jnp.where(here, cosine, -sine), rows[1], jnp.where(here, -sine, cosine)


def turn_diagonal(ff, bb, fb, matrix):
    m00, m01, m10, m11 = matrix
    return (
        m00 * m00 * ff + 2.0 * m00 * m01 * fb + m01 * m01 * bb,
        m10 * m10 * ff + 2.0 * m10 * m11 * fb + m11 * m11 * bb,
        m00 * m10 * ff + (m00 * m11 + m01 * m10) * fb + m01 * m11 * bb,
    )


def turn_block(block, left, right):
    ff, fb, bf, bb = block
    ff, bf = turn(ff, bf, left)
    fb, bb = turn(fb, bb, left)
    ff, fb = turn(ff, fb, right)
    bf, bb = turn(bf, bb, right)
    return ff, fb, bf, bb


def shifted(matrix, by):
    return [roll(m, -by) for m in matrix]


def three_matrices(packed):
    rows = unpack(packed)
    lane = lanes_of(rows[0])
    left = lane < LANES
    first = matrix_of(*rows[:3], left, 0)
    ff, bb, fb = turn_diagonal(*rows[:3], first)
    near_ff, near_fb, _, near_bb = turn_block(rows[3:7], first, shifted(first, 1))
    _, far_fb, _, _ = turn_block(rows[7:11], first, shifted(first, 2))
    diagonal = ff, roll(bb, -1), near_fb
    second = matrix_of(*diagonal, left, HALF - 1)
    block = near_ff, far_fb, roll(fb, -1), roll(near_bb, -1)
    ff, bb, _ = turn_diagonal(*diagonal, second)
    _, cross, _, _ = turn_block(block, second, shifted(second, 1))
    upper_ahead = (lane < LANES - 1) | (lane == HALF - 1)
    return first, second, matrix_of(ff, roll(bb, -1), cross, upper_ahead, None)


def ordered_sum(x):
    return functools.reduce(jnp.add, [x[i] for i in range(x.shape[0])])


def chosen(condition, x, y):
    return jnp.where(condition, x, y)


def wide(matrices, index=0):
    row = slice(index, index + 1)
    return [[jnp.broadcast_to(v[row], (CHUNK, HALF)) for v in matrix] for matrix in matrices]


def rotated(top, bottom, matrices):
    first, second, third = matrices
    ahead, back = turn(*split(top, bottom), first)
    ahead, back = turn(ahead, roll(back, -1), second)
    ahead, back = turn(ahead, roll(back, -1), third)
    ahead, back = swap_at(HALF - 1, ahead, roll(back, 1))
    return split(*swap_at(0, ahead, roll(back, 1)))


def chunks(ref):
    return [pl.ds(start, CHUNK) for start in range(0, ref.shape[0], CHUNK)]


def start_kernel(place_ref, work_ref, top_ref, bottom_ref, band_ref):
    def read(start):
        row = pl.ds(start, CHUNK)
        top = to_cycle(work_ref[row, :HALF])
        bottom = reverse(to_cycle(work_ref[row, HALF:]))
        top_ref[row, :] = top
        bottom_ref[row, :] = bottom
        return top, bottom

    band_ref[...] = pack(bands_of(read, work_ref.shape[0]))


def rotate_kernel(place_ref, top_ref, bottom_ref, parts_ref, kept_ref, odd_ref, even_ref):
    place = place_ref[0, 0]
    at_odd = place % 2 == 1
    matrices = wide(three_matrices(ordered_sum(parts_ref)))
    for row in chunks(top_ref):
        top, bottom = rotated(top_ref[row, :], bottom_ref[row, :], matrices)
        right = chosen(place == 0, reverse(bottom), top)
        kept_ref[row, :] = chosen(place == 0, top, reverse(top))
        odd_ref[row, :] = chosen(at_odd, right, bottom)
        even_ref[row, :] = chosen(at_odd, bottom, right)


def arrive_kernel(count, place_ref, kept_ref, odd_ref, even_ref, top_ref, bottom_ref, band_ref):
    place = place_ref[0, 0]
    at_odd = place % 2 == 1

    def read(start):
        row = pl.ds(start, CHUNK)
        kept, odd, even = kept_ref[row, :], odd_ref[row, :], even_ref[row, :]
        top = chosen(place == 0, kept, chosen(at_odd, even, odd))
        bottom = chosen(place == count - 1, kept, chosen(at_odd, odd, even))
        top_ref[row, :] = top
        bottom_ref[row, :] = bottom
        return top, bottom

    band_ref[...] = pack(bands_of(read, kept_ref.shape[0]))


def rotate_far_kernel(count, place_ref, top_ref, bottom_ref, parts_ref, x_ref, y_ref, late_ref):
    place = place_ref[0, 0]
    low = place % 4 < 2
    matrices = wide(three_matrices(ordered_sum(parts_ref)))
    for row in chunks(top_ref):
        top, bottom = rotated(top_ref[row, :], bottom_ref[row, :], matrices)
        flip = reverse(chosen(place == 0, bottom, top))
        upper = chosen((place == 0) | (place == count - 1), flip, top)
        lower = chosen(place == 0, top, bottom)
        x = chosen(low, upper, lower)
        x_ref[row, :] = x
        y_ref[row, :] = chosen(low, lower, upper)
        late_ref[row, :] = x


def late_edges(count):
    middle = count // 2
    return [(middle, middle + 2), (middle - 1, middle - 3)]


def arrive_far_kernel(count, place_ref, x_ref, y_ref, late_ref, x_in_ref, y_in_ref, late_in_ref, *refs):
    before_refs, after_refs, band_ref = refs[:2], refs[2:4], refs[4]
    place = place_ref[0, 0]
    low = place % 4 < 2
    start_end, last_end = place == 0, place == count - 1
    late = functools.reduce(jnp.logical_or, [place == i for i in sum(late_edges(count), ())])

    def read_before(start):
        row = pl.ds(start, CHUNK)
        x, y, y_in = x_ref[row, :], y_ref[row, :], y_in_ref[row, :]
        x_in = chosen(late, late_in_ref[row, :], x_in_ref[row, :])
        top = chosen(start_end, y, chosen(low, y_in, x_in))
        bottom = chosen(start_end, y_in, chosen(low, y, x))
        before_refs[0][row, :] = top
        before_refs[1][row, :] = bottom
        return top, bottom

    def read_after(start):
        row = pl.ds(start, CHUNK)
        x, y, y_in = x_ref[row, :], y_ref[row, :], y_in_ref[row, :]
        x_in = chosen(late, late_in_ref[row, :], x_in_ref[row, :])
        top = chosen(low, x, chosen(last_end, y_in, y))
        bottom = chosen(low, x_in, chosen(last_end, y, y_in))
        after_refs[0][row, :] = top
        after_refs[1][row, :] = bottom
        return top, bottom

    rows = x_ref.shape[0]
    band_ref[...] = pack(bands_of(read_before, rows), bands_of(read_after, rows))


def finish_kernel(
    count, place_ref, top_before_ref, bottom_before_ref, top_after_ref, bottom_after_ref, parts_ref,
    out_hbm, out_ref, sems
):
    place = place_ref[0, 0]
    both = three_matrices(ordered_sum(parts_ref))
    matrices_before, matrices_after = wide(both, 0), wide(both, 1)
    size = out_ref.shape[0] // sems.shape[0]
    copies = []
    for i in range(sems.shape[0]):
        for start in range(i * size, (i + 1) * size, CHUNK):
            row = pl.ds(start, CHUNK)
            top, bottom = rotated(top_before_ref[row, :], bottom_before_ref[row, :], matrices_before)
            out_ref[row, :HALF] = from_cycle(chosen(place == 1, reverse(bottom), top))
            top, bottom = rotated(top_after_ref[row, :], bottom_after_ref[row, :], matrices_after)
            out_ref[row, HALF:] = from_cycle(chosen(place == count - 1, top, reverse(bottom)))
        part = pl.ds(i * size, size)
        copies.append(pltpu.make_async_copy(out_ref.at[part], out_hbm.at[part], sems.at[i]))
        copies[-1].start()
    for copy in copies:
        copy.wait()


def call(kernel, inputs, outputs, scratch=(), space=pltpu.VMEM):
    spec = pl.BlockSpec(memory_space=pltpu.VMEM)
    return pl.pallas_call(
        kernel,
        in_specs=[pl.BlockSpec(memory_space=pltpu.SMEM)] + [spec] * (len(inputs) - 1),
        out_specs=[pl.BlockSpec(memory_space=space)] * len(outputs),
        out_shape=[jax.ShapeDtypeStruct(shape, jnp.float32) for shape in outputs],
        scratch_shapes=list(scratch),
        compiler_params=pltpu.CompilerParams(vmem_limit_bytes=8 * 1024 * 1024),
    )(*inputs)


def from_all(x, axes, first=0):
    count = lax.axis_size(axes)
    copies = jnp.broadcast_to(x[None], (count, *x.shape))
    order = [(first + i) % count for i in range(count)]
    groups = [order] if first else None
    return lax.all_to_all(copies, axes, 0, 0, tiled=True, axis_index_groups=groups)


def row_parts(x):
    near = ordered_sum(from_all(x, ("half", "near")))
    return from_all(near, "far", lax.axis_size("far") // 2 + 1)


def exchange(x, edges):
    return lax.ppermute(x, "pair", edges + [(j, i) for i, j in edges])


def per_device(snapshots):
    rows = snapshots.shape[0]
    count = lax.axis_size("pair")
    place = lax.axis_index("pair").astype(jnp.int32).reshape(1, 1)
    block, packed = (rows, HALF), (PACKED_ROWS, LANES)
    line = list(range(count))
    odd_edges, even_edges = list(zip(line[1:-1:2], line[2::2])), list(zip(line[::2], line[1::2]))
    cycle = line[::2] + line[::-2]
    x_edges = list(zip(cycle[::2], cycle[1::2]))
    y_edges = list(zip(cycle[1::2], cycle[2::2] + cycle[:1]))

    top, bottom, band = call(start_kernel, [place, snapshots], [block, block, packed])
    kept, odd, even = call(
        rotate_kernel, [place, top, bottom, row_parts(band)], [block] * 3
    )
    top, bottom, band = call(
        functools.partial(arrive_kernel, count),
        [place, kept, exchange(odd, odd_edges), exchange(even, even_edges)],
        [block, block, packed],
    )
    x, y, late = call(
        functools.partial(rotate_far_kernel, count),
        [place, top, bottom, row_parts(band)],
        [block] * 3,
    )
    x_in = exchange(x, [edge for edge in x_edges if edge not in late_edges(count)])
    y_in = exchange(y, y_edges)
    late_in = exchange(late, late_edges(count))
    *blocks, band = call(
        functools.partial(arrive_far_kernel, count),
        [place, x, y, late, x_in, y_in, late_in],
        [block] * 4 + [(2 * PACKED_ROWS, LANES)],
    )
    (out,) = call(
        functools.partial(finish_kernel, count),
        [place, *blocks, row_parts(band)],
        [(rows, 2 * HALF)],
        [pltpu.VMEM((rows, 2 * HALF), jnp.float32), pltpu.SemaphoreType.DMA((4,))],
        pltpu.HBM,
    )
    return out


def solution(mesh):
    pairs, rows = mesh.devices.shape
    fine = Mesh(mesh.devices.reshape(pairs, 2, rows // 4, 2), ("pair", "half", "far", "near"))
    spec = P(("half", "far", "near"), "pair")
    return jax.shard_map(
        per_device, mesh=fine, in_specs=(spec,), out_specs=spec, check_vma=False
    )
```
